32 devices in a mesh: groups: 2 (over y), tok: 16 (over z, x, core), feat: 1.
Axes of the slice: x: 2, y: 2, z: 4, core: 2. Of those that a mesh axis runs over, the one named last changes fastest.
Arguments:
- activations: bfloat16 [8192, 16384], P(('groups', 'tok'), 'feat'), parts along dimension 0, may hold values from -200 to 200, as said below
- sketch: bfloat16 [1, 16384, 128], P('feat', 'tok'), may hold values from -0.046875 to 0.046875
Outputs:
- basis: float32 [2, 16384, 128], P(('groups', 'feat'), 'tok'), parts along dimension 0
- coords: float32 [8192, 128], P(('groups', 'tok')), parts along dimension 0
- resid_rms: float32 [8192], P(('groups', 'tok')), parts along dimension 0
The draws below stay inside these ranges and needn't reach their ends.
There are 2 independent parts, one for each index of `groups`. The reference program is written for one: setup_inputs(seed, part) draws one part's arguments, and reference() takes and returns one part's arrays. A program takes and returns all parts, laid end to end along the dimension named above; an argument that names none is the same for every part. Nothing has to cross between parts.
Inputs may be any that keep to these rules, and one draw needn't show every extreme that they name: real-valued activations.
All inputs are finite; a program needn't handle non-finite values.
Results may differ from the reference program's by a relative error of at most 0.0027.
Values may be sent and summed in bfloat16 or wider, within the bound.
No kernel may reach another device: no remote copies, remote signals or barrier semaphores. Data moves between devices by JAX's collectives and lax.ppermute only.
A program may use at most 64 MiB of HBM per device.

```python
import math
import jax
import jax.numpy as jnp
from jax import lax

D = 16384
R = 128
TOK_DEV = 256
TOKENS = 4096
HALVES = 1
FSHARD = 16384
N_TOK = 16


def draw_activations(key, part):
    key = jax.random.fold_in(key, 11)
    noise_key, column_key, row_key = jax.random.split(key, 3)
    column_scale = jnp.exp(jax.random.uniform(column_key, (D,), jnp.float32, math.log(0.3), math.log(3.0)))
    row_scale = jnp.exp(jax.random.uniform(row_key, (TOKENS,), jnp.float32, math.log(0.3), math.log(3.0)))
    positions = jnp.arange(TOKENS, dtype=jnp.float32) / jnp.float32(max(TOKENS - 1, 1))
    row_scale = row_scale * jnp.exp(math.log(3.0) * positions)
    values = jax.random.truncated_normal(noise_key, -6.0, 6.0, (TOKENS, D), jnp.float32)
    return (values * row_scale[:, None] * column_scale[None, :]).astype(jnp.bfloat16)


def steps_of(own_key, shape, pieces, least, largest):
    level, own = 1.0, jax.random.fold_in(own_key, 6)
    for dim, shards_of in pieces:
        steps = jnp.exp(jax.random.uniform(jax.random.fold_in(own, dim), (shards_of,), jnp.float32, least / len(pieces), largest / len(pieces)))
        level = level * jnp.repeat(steps, shape[dim] // shards_of).reshape([-1 if axis == dim else 1 for axis in range(len(shape))])
    return level


def gaussian(own_key, dims, scale, limit, cuts=(), kind=jnp.bfloat16):
    gain = steps_of(own_key, dims, cuts, -0.22, 0.18) if cuts else 1.0
    array = jax.random.normal(own_key, dims, jnp.float32) * scale * gain
    return jnp.minimum(jnp.maximum(array, -limit), limit).astype(kind)


def setup_inputs(seed: int = 0, part: int = 0) -> dict:
    arg_keys = jax.random.split(jax.random.key(seed), 3)
    part_splits = jax.random.split(jax.random.fold_in(arg_keys[2], part), 3)
    return {
        "activations": draw_activations(jax.random.fold_in(jax.random.fold_in(arg_keys[2], part), 71), part),
        "sketch": gaussian(arg_keys[1], (HALVES, FSHARD, R), D ** -0.5, 0.046875, ((1, 16),)),
    }


def reference(activations, sketch):
    sketch_flat = sketch.reshape(D, R)
    sketched = jnp.dot(activations.astype(jnp.float32), sketch_flat.astype(jnp.float32), preferred_element_type=jnp.float32).astype(jnp.bfloat16)
    range_full = jnp.dot(activations.T.astype(jnp.float32), sketched.astype(jnp.float32), preferred_element_type=jnp.float32)
    gram_matrix = jnp.dot(range_full.T.astype(jnp.float32), range_full.astype(jnp.float32), preferred_element_type=jnp.float32, precision=lax.Precision.HIGHEST)
    factor = jnp.linalg.cholesky(gram_matrix)
    ortho = jax.scipy.linalg.solve_triangular(factor, range_full.T, lower=True).T
    basis = (ortho * jnp.float32(math.sqrt(D))).reshape(HALVES, FSHARD, R)
    ortho_b = ortho.astype(jnp.bfloat16)
    coords = jnp.dot(activations.astype(jnp.float32), ortho_b.astype(jnp.float32), preferred_element_type=jnp.float32)
    coords_b = coords.astype(jnp.bfloat16)

    def block_energy(inputs_pair):
        token_block, coord_block = inputs_pair
        rebuilt = jnp.dot(coord_block.astype(jnp.float32), ortho_b.T.astype(jnp.float32), preferred_element_type=jnp.float32)
        leftover = token_block.astype(jnp.float32) - rebuilt
        return lax.optimization_barrier(jnp.sum(leftover * leftover, axis=1))
    energy = lax.map(block_energy, (activations.reshape(N_TOK, TOK_DEV, D), coords_b.reshape(N_TOK, TOK_DEV, R)))
    energy = energy.reshape(TOKENS)
    resid_rms = jnp.sqrt(energy / D + 1e-06)
    return (basis, coords, resid_rms)
```

```python
import functools
import math

import jax
import jax.numpy as jnp
from jax import lax
from jax.experimental import pallas as pl
from jax.experimental.pallas import tpu as pltpu
from jax.sharding import PartitionSpec as P

F32, BF16 = jnp.float32, jnp.bfloat16
HIGH = lax.Precision.HIGHEST
ARB = pltpu.CompilerParams(dimension_semantics=("arbitrary",), vmem_limit_bytes=48 * 2**20)

X_BIT, ZLO, ZHI = 1, 2, 4
NEAR_A, FAR_A = (0, 4, 2, 6), (1, 5, 3, 7)
NEAR_B, FAR_B = (0, 4, 1, 5), (2, 6, 3, 7)


def swap(value, bit, n):
    return lax.ppermute(value, "tok", [(i, i ^ bit) for i in range(n)])


def encode(value):
    return (value * jnp.abs(value)).astype(BF16)


def decode(coded):
    wide = coded.astype(F32)
    root = jnp.sqrt(jnp.abs(wide))
    return jnp.where(wide < 0, -root, root)


def split_kernel(core_ref, x_ref, other_ref, norm_ref, acc_ref):
    step = pl.program_id(0)
    width = other_ref.shape[1]
    start = pl.multiple_of((1 - core_ref[0]) * width, width)
    other_ref[...] = x_ref[:, pl.ds(start, width)]
    wide = x_ref[...].astype(F32)
    square = wide * wide
    total = square[:, :128]
    for i in range(1, 2 * width // 128):
        total = total + square[:, i * 128 : (i + 1) * 128]

    @pl.when(step == 0)
    def _():
        acc_ref[...] = total

    @pl.when(step > 0)
    def _():
        acc_ref[...] += total

    @pl.when(step == pl.num_programs(0) - 1)
    def _():
        norm_ref[...] = jnp.sum(acc_ref[...], axis=1, keepdims=True)


def split(core, x, width):
    rows, features = x.shape
    return pl.pallas_call(
        split_kernel,
        grid_spec=pltpu.PrefetchScalarGridSpec(
            num_scalar_prefetch=1,
            grid=(features // (2 * width),),
            in_specs=[pl.BlockSpec((rows, 2 * width), lambda i, s: (0, i))],
            out_specs=[
                pl.BlockSpec((rows, width), lambda i, s: (0, i)),
                pl.BlockSpec((rows, 1), lambda i, s: (0, 0)),
            ],
            scratch_shapes=[pltpu.VMEM((rows, 128), F32)],
        ),
        out_shape=[
            jax.ShapeDtypeStruct((rows, features // 2), BF16),
            jax.ShapeDtypeStruct((rows, 1), F32),
        ],
        compiler_params=ARB,
        cost_estimate=pl.CostEstimate(flops=2 * rows * features, bytes_accessed=3 * rows * features, transcendentals=0),
    )(core, x)


def x_specs(rows, half):
    return [
        pl.BlockSpec((rows, half), functools.partial(lambda k, i, s: (0, s[k, i]), k)) for k in range(4)
    ]


def project_kernel(has_init, table_ref, xa, xb, oa, ob, sa, sb, *rest):
    init_ref, out_ref = rest if has_init else (None, rest[0])
    rows = xa.shape[0]
    own = jnp.dot(xa[...], sa[...], preferred_element_type=F32) + jnp.dot(xb[...], sb[...], preferred_element_type=F32)
    other = jnp.dot(oa[...], sa[...], preferred_element_type=F32) + jnp.dot(ob[...], sb[...], preferred_element_type=F32)
    first = pl.program_id(0) == 0

    @pl.when(first)
    def _():
        out_ref[:rows, :] = own + (init_ref[:rows, :] if has_init else 0.0)
        out_ref[rows:, :] = other + (init_ref[rows:, :] if has_init else 0.0)

    @pl.when(jnp.logical_not(first))
    def _():
        out_ref[:rows, :] += own
        out_ref[rows:, :] += other


def project(table, x, other, sa, sb, init=None):
    rows, half, rank = x.shape[0], sa.shape[0] // 4, sa.shape[1]
    rows_spec = pl.BlockSpec((half, rank), lambda i, s: (i, 0))
    whole = pl.BlockSpec((2 * rows, rank), lambda i, s: (0, 0))
    return pl.pallas_call(
        functools.partial(project_kernel, init is not None),
        grid_spec=pltpu.PrefetchScalarGridSpec(
            num_scalar_prefetch=1,
            grid=(4,),
            in_specs=x_specs(rows, half) + [rows_spec, rows_spec] + ([whole] if init is not None else []),
            out_specs=whole,
        ),
        out_shape=jax.ShapeDtypeStruct((2 * rows, rank), F32),
        compiler_params=ARB,
        cost_estimate=pl.CostEstimate(
            flops=2 * 2 * rows * 8 * half * rank, bytes_accessed=2 * 2 * rows * 8 * half, transcendentals=0
        ),
    )(table, x, x, other, other, sa, sb, *([init] if init is not None else []))


def spread_kernel(coded, table_ref, xa, xb, oa, ob, y_ref, za, zb):
    rows = xa.shape[0]
    for own, other, out in ((xa, oa, za), (xb, ob, zb)):
        term = lax.dot_general(
            own[...], y_ref[:rows, :], (((0,), (0,)), ((), ())), preferred_element_type=F32
        ) + lax.dot_general(other[...], y_ref[rows:, :], (((0,), (0,)), ((), ())), preferred_element_type=F32)
        out[...] = encode(term) if coded else term


def spread(table, x, other, y, half, coded):
    rows, rank = x.shape[0], y.shape[1]
    rows_spec = pl.BlockSpec((half, rank), lambda i, s: (i, 0))
    shape = jax.ShapeDtypeStruct((4 * half, rank), BF16 if coded else F32)
    return pl.pallas_call(
        functools.partial(spread_kernel, coded),
        grid_spec=pltpu.PrefetchScalarGridSpec(
            num_scalar_prefetch=1,
            grid=(4,),
            in_specs=x_specs(rows, half) + [pl.BlockSpec((2 * rows, rank), lambda i, s: (0, 0))],
            out_specs=[rows_spec, rows_spec],
        ),
        out_shape=[shape, shape],
        compiler_params=ARB,
        cost_estimate=pl.CostEstimate(
            flops=2 * 2 * rows * 8 * half * rank, bytes_accessed=2 * 2 * rows * 8 * half, transcendentals=0
        ),
    )(table, x, x, other, other, y)


def gather(piece, bits, n):
    held = piece
    for bit in bits[:-1]:
        held = jnp.concatenate([held, swap(held, 2 * bit, n)], axis=0)
    return held, swap(held, 2 * bits[-1], n)


def reduce(kept, sent, bits, n):
    for bit in bits:
        total = kept + decode(swap(sent, 2 * bit, n))
        if bit != bits[-1]:
            size = total.shape[0] // 2
            kept, sent = total[:size], encode(total[size:])
    return total


def shards(n, activations, sketch):
    x, rows = activations, activations.shape[0]
    width, rank = sketch.shape[1], sketch.shape[2]
    half = width // 2
    depth = n * width
    own = sketch[0]
    index = lax.axis_index("tok")
    core = index % 2

    def table(list_a, list_b):
        a = jnp.bitwise_xor(index, 2 * jnp.array(list_a, jnp.int32))
        b = jnp.bitwise_xor(index, 2 * jnp.array(list_b, jnp.int32))
        return jnp.stack([2 * a, 2 * b + 1, a // 2 * 2, b // 2 * 2 + 1]).astype(jnp.int32)

    near, far = table(NEAR_A, NEAR_B), table(FAR_A, FAR_B)

    with jax.named_scope("gather_sketch"):
        near_a, far_a = gather(own[:half], (ZHI, ZLO, X_BIT), n)
        near_b, far_b = gather(own[half:], (ZHI, X_BIT, ZLO), n)
    with jax.named_scope("split_features"):
        outgoing, norm = split(core.reshape(1).astype(jnp.int32), x, width)
        other = swap(outgoing, 1, n)
    with jax.named_scope("sketched"):
        part = project(near, x, other, near_a, near_b)
        part = project(far, x, other, far_a, far_b, part)
        theirs = swap(part, 1, n)
        sketched = (part + jnp.concatenate([theirs[rows:], theirs[:rows]])).astype(BF16)
    with jax.named_scope("range"):
        sent_a, sent_b = spread(far, x, other, sketched, half, True)
        kept_a, kept_b = spread(near, x, other, sketched, half, False)
        range_a = reduce(kept_a, sent_a, (X_BIT, ZLO, ZHI), n)
        range_b = reduce(kept_b, sent_b, (ZLO, X_BIT, ZHI), n)
        range_rows = jnp.concatenate([range_a, range_b], axis=0)
    with jax.named_scope("gather_range"):
        near_a, far_a = gather(range_a.astype(BF16), (ZHI, ZLO, X_BIT), n)
        near_b, far_b = gather(range_b.astype(BF16), (ZHI, X_BIT, ZLO), n)
    with jax.named_scope("gram"):
        gram = jnp.dot(range_rows.T, range_rows, preferred_element_type=F32, precision=HIGH)
        for bit in (1, 2, 4, 8):
            gram = gram + swap(gram, bit, n)
    with jax.named_scope("factor"):
        factor = jnp.linalg.cholesky(gram)
        inverse = jax.scipy.linalg.solve_triangular(factor, jnp.eye(rank, dtype=F32), lower=True)
        basis = jnp.dot(range_rows, inverse.T, precision=HIGH) * F32(math.sqrt(depth))
    with jax.named_scope("coords"):
        part = project(near, x, other, near_a, near_b)
        part = project(far, x, other, far_a, far_b, part)
        raw = part[:rows] + swap(part[rows:], 1, n)
        coords = jnp.dot(raw, inverse.T, precision=HIGH)
    with jax.named_scope("residual"):
        lost = coords - coords.astype(BF16).astype(F32)
        energy = norm[:, 0] + jnp.sum(lost * lost - coords * coords, axis=1)
        resid_rms = jnp.sqrt(jnp.maximum(energy, 0.0) / depth + 1e-06)
    return basis[None], coords, resid_rms


def shards_any(depth, activations, sketch):
    sketch_all = lax.all_gather(sketch, "tok", axis=1, tiled=True)[0]
    sketched = lax.psum(jnp.dot(activations, sketch_all, preferred_element_type=F32), "feat").astype(BF16)
    term = lax.dot_general(activations, sketched, (((0,), (0,)), ((), ())), preferred_element_type=F32)
    range_rows = lax.psum_scatter(term, "tok", scatter_dimension=0, tiled=True)
    gram = jnp.dot(range_rows.T, range_rows, preferred_element_type=F32, precision=HIGH)
    factor = jnp.linalg.cholesky(lax.psum(gram, ("tok", "feat")))
    own_rows = jax.scipy.linalg.solve_triangular(factor, range_rows.T, lower=True).T
    half_basis = lax.all_gather(own_rows.astype(BF16), "tok", axis=0, tiled=True)
    basis = (own_rows * F32(math.sqrt(depth)))[None]
    coords = lax.psum(jnp.dot(activations, half_basis, preferred_element_type=F32), "feat")
    rebuilt = jnp.dot(coords.astype(BF16), half_basis.T, preferred_element_type=F32)
    leftover = activations.astype(F32) - rebuilt
    energy = lax.psum(jnp.sum(leftover * leftover, axis=1), "feat")
    return basis, coords, jnp.sqrt(energy / depth + 1e-06)


def solution(mesh):
    n, feat = mesh.shape["tok"], mesh.shape["feat"]

    def call(activations, sketch):
        depth = activations.shape[1]
        if n == 16 and feat == 1:
            body = functools.partial(shards, n)
        else:
            body = functools.partial(shards_any, depth)
        return jax.shard_map(
            body,
            mesh=mesh,
            in_specs=(P(("groups", "tok"), "feat"), P("feat", "tok", None)),
            out_specs=(
                P(("groups", "feat"), "tok", None),
                P(("groups", "tok"), None),
                P(("groups", "tok")),
            ),
            check_vma=False,
        )(activations, sketch)

    return call
```

```python
import functools
import math

import jax
import jax.numpy as jnp
from jax import lax
from jax.experimental import pallas as pl
from jax.experimental.pallas import tpu as pltpu
from jax.sharding import PartitionSpec as P

F32, BF16 = jnp.float32, jnp.bfloat16
HIGH = lax.Precision.HIGHEST
VMEM = pl.BlockSpec(memory_space=pltpu.VMEM)
SMEM = pl.BlockSpec(memory_space=pltpu.SMEM)
ANY = pl.BlockSpec(memory_space=pl.ANY)
PARAMS = pltpu.CompilerParams(vmem_limit_bytes=10 * 2**20)

X_BIT, ZLO, ZHI = 1, 2, 4
HLX, HXL, LHX = (ZHI, ZLO, X_BIT), (ZHI, X_BIT, ZLO), (ZLO, ZHI, X_BIT)
PIECES = ((4, HLX), (4, HXL))
LOADS, PARTS = 8, 4


def swap(value, bit, n):
    return lax.ppermute(value, "tok", [(i, i ^ bit) for i in range(n)])


def owners(bits):
    near = [0]
    for bit in bits[:-1]:
        near += [owner ^ bit for owner in near]
    return near, [owner ^ bits[-1] for owner in near]


def encode(value):
    return (value * jnp.abs(value)).astype(BF16)


def decode(coded):
    wide = coded.astype(F32)
    root = jnp.sqrt(jnp.abs(wide))
    return jnp.where(wide < 0, -root, root)


def after(value, *earlier):
    return lax.optimization_barrier((value, *earlier))[0]


def pinned(value):
    return pltpu.with_memory_space_constraint(value, pltpu.VMEM)


def load_kernel(width, core_ref, x_ref, copy_ref, norm_ref, *refs):
    outs, sems = refs[:-1], refs[-1]
    rows, features = x_ref.shape
    chunk = rows // LOADS

    def copy(i):
        part = pl.ds(i * chunk, chunk)
        return pltpu.make_async_copy(x_ref.at[part, :], copy_ref.at[part, :], sems.at[i])

    for i in range(LOADS):
        copy(i).start()
    for i in range(LOADS):
        copy(i).wait()
        out = outs[i * len(outs) // LOADS]
        base = i * chunk % out.shape[0]
        for k in range(features // (2 * width)):
            start = pl.multiple_of((2 * k + 1 - core_ref[0]) * width, width)
            out[base : base + chunk, k * width : (k + 1) * width] = copy_ref[
                i * chunk : (i + 1) * chunk, pl.ds(start, width)
            ]
        total = jnp.zeros((chunk, 128), F32)
        for k in range(0, features, 128):
            wide = copy_ref[i * chunk : (i + 1) * chunk, k : k + 128].astype(F32)
            total = total + wide * wide
        norm_ref[i * chunk : (i + 1) * chunk, :] = total


def load(core, x, width):
    rows, features = x.shape
    part = (rows // PARTS, features // 2)
    return pl.pallas_call(
        functools.partial(load_kernel, width),
        in_specs=[SMEM, ANY],
        out_specs=[VMEM] * (2 + PARTS),
        out_shape=[pltpu.VMEM(x.shape, BF16), pltpu.VMEM((rows, 128), F32)] + [pltpu.VMEM(part, BF16)] * PARTS,
        scratch_shapes=[pltpu.SemaphoreType.DMA((LOADS,))],
        compiler_params=PARAMS,
        cost_estimate=pl.CostEstimate(flops=2 * rows * features, bytes_accessed=4 * rows * features, transcendentals=0),
    )(core, pltpu.with_memory_space_constraint(x, pltpu.HBM))


def tokens(x_ref, other_refs, table_ref, row, step, j, size):
    mine = x_ref[:, pl.ds(pl.multiple_of(table_ref[row, j] * 128, 128), size)]
    start = pl.multiple_of(table_ref[row + step, j] * 128, 128)
    return jnp.concatenate([mine] + [ref[:, pl.ds(start, size)] for ref in other_refs], axis=0)


def project_kernel(n_pieces, has_init, table_ref, x_ref, *refs):
    others, refs, out_ref = refs[:PARTS], refs[PARTS:-1], refs[-1]
    pieces = refs[:n_pieces]
    total = refs[n_pieces][...] if has_init else None
    for j in range(4):
        sizes = [piece.shape[0] // 4 for piece in pieces]
        block = jnp.concatenate([ref[j * size : (j + 1) * size, :] for ref, size in zip(pieces, sizes)], axis=0)
        left = jnp.concatenate(
            [tokens(x_ref, others, table_ref, p, n_pieces, j, size) for p, size in enumerate(sizes)], axis=1
        )
        term = jnp.dot(left, block, preferred_element_type=F32)
        total = term if total is None else total + term
    out_ref[...] = total


def project(table, x, others, pieces, init=None):
    rows, rank = x.shape[0], pieces[0].shape[1]
    depth = sum(piece.shape[0] for piece in pieces)
    extra = [] if init is None else [init]
    return pl.pallas_call(
        functools.partial(project_kernel, len(pieces), init is not None),
        in_specs=[SMEM] + [VMEM] * (1 + PARTS + len(pieces) + len(extra)),
        out_specs=VMEM,
        out_shape=jax.ShapeDtypeStruct((2 * rows, rank), F32),
        compiler_params=PARAMS,
        cost_estimate=pl.CostEstimate(
            flops=4 * rows * depth * rank, bytes_accessed=4 * rows * depth, transcendentals=0
        ),
    )(table, pinned(x), *map(pinned, others), *pieces, *extra)


def spread_kernel(coded, n_pieces, table_ref, x_ref, *refs):
    others, y_ref, outs = refs[:PARTS], refs[PARTS], refs[PARTS + 1 :]
    turned = y_ref[...].astype(F32).T.astype(BF16)
    for p, out in enumerate(outs):
        size = out.shape[0] // 4
        for j in range(4):
            term = jnp.dot(
                turned, tokens(x_ref, others, table_ref, p, n_pieces, j, size), preferred_element_type=F32
            ).T
            out[j * size : (j + 1) * size, :] = encode(term) if coded else term


def spread(table, x, others, y, sizes, coded):
    rows, rank = x.shape[0], y.shape[1]
    return pl.pallas_call(
        functools.partial(spread_kernel, coded, len(sizes)),
        in_specs=[SMEM] + [VMEM] * (2 + PARTS),
        out_specs=[VMEM] * len(sizes),
        out_shape=[jax.ShapeDtypeStruct((4 * size, rank), BF16 if coded else F32) for size in sizes],
        compiler_params=PARAMS,
        cost_estimate=pl.CostEstimate(
            flops=16 * rows * sum(sizes) * rank, bytes_accessed=16 * rows * sum(sizes), transcendentals=0
        ),
    )(table, pinned(x), *map(pinned, others), y)


def factor_kernel(scale, gram_ref, range_ref, out_ref, basis_ref):
    n, b = gram_ref.shape[0], 8
    lane = lax.broadcasted_iota(jnp.int32, (b, n), 1)
    sub = lax.broadcasted_iota(jnp.int32, (b, n), 0)

    def full(value):
        return jnp.broadcast_to(value, (b, n))

    tiles = [gram_ref[b * i : b * i + b, :] for i in range(n // b)]
    for t in range(n // b):
        k = b * t
        group = (lane >= k) & (lane < k + b)
        cols = [full(tiles[t][:, k + c : k + c + 1]) for c in range(b)]
        entry = {(r, c): full(cols[c][r : r + 1, :]) for r in range(b) for c in range(r + 1)}
        rows = [jnp.where(lane == k + r, 1.0, jnp.where(group, 0.0, full(tiles[t][r : r + 1, :]))) for r in range(b)]
        invs, low = [], {}
        for c in range(b):
            invs.append(1.0 / entry[c, c])
            for r in range(c + 1, b):
                low[r, c] = entry[r, c] * invs[c]
            for r in range(c + 1, b):
                for s in range(c + 1, r + 1):
                    entry[r, s] = entry[r, s] - low[r, c] * entry[s, c]
            for r in range(c + 1, b):
                rows[r] = rows[r] - low[r, c] * rows[c]
        solved = [row * inv for row, inv in zip(rows, invs)]
        for c in range(b - 1, 0, -1):
            for r in range(c):
                solved[r] = solved[r] - low[c, r] * solved[c]
        for i in range(t + 1, n // b):
            new = jnp.where(group, 0.0, tiles[i])
            for c in range(b):
                new = new - full(tiles[i][:, k + c : k + c + 1]) * solved[c]
            tiles[i] = new
        done, pivots = rows[0], entry[0, 0]
        for r in range(1, b):
            done = jnp.where(sub == r, rows[r], done)
            pivots = jnp.where(sub == r, entry[r, r], pivots)
        out_ref[k : k + b, :] = jnp.where(lane <= k + sub, done, 0.0) * lax.rsqrt(pivots)
    basis_ref[...] = scale * lax.dot_general(
        range_ref[...], out_ref[...], (((1,), (1,)), ((), ())), precision=HIGH, preferred_element_type=F32
    )


def factored(scale, gram, range_rows):
    return pl.pallas_call(
        functools.partial(factor_kernel, scale),
        in_specs=[VMEM] * 2,
        out_specs=[VMEM] * 2,
        out_shape=[jax.ShapeDtypeStruct(gram.shape, F32), jax.ShapeDtypeStruct(range_rows.shape, F32)],
        compiler_params=PARAMS,
        cost_estimate=pl.CostEstimate(flops=10**7, bytes_accessed=2 * 10**7, transcendentals=0),
    )(gram, range_rows)


def close_kernel(depth, part_ref, theirs_ref, inverse_ref, norm_ref, coords_ref, resid_ref):
    raw = part_ref[: theirs_ref.shape[0], :] + theirs_ref[...]
    coords = lax.dot_general(raw, inverse_ref[...], (((1,), (1,)), ((), ())), precision=HIGH)
    coords_ref[...] = coords
    lost = coords - coords.astype(BF16).astype(F32)
    terms = norm_ref[...] + (lost * lost - coords * coords)
    energy = jnp.sum(terms.T, axis=0, keepdims=True)
    resid_ref[...] = jnp.sqrt(jnp.maximum(energy, 0.0) / depth + 1e-06)


def close(depth, part, theirs, inverse, norm):
    rows, rank = theirs.shape
    return pl.pallas_call(
        functools.partial(close_kernel, depth),
        in_specs=[VMEM] * 4,
        out_specs=[VMEM] * 2,
        out_shape=[jax.ShapeDtypeStruct((rows, rank), F32), jax.ShapeDtypeStruct((1, rows), F32)],
        compiler_params=PARAMS,
        cost_estimate=pl.CostEstimate(flops=2 * rows * rank * rank, bytes_accessed=16 * rows * rank, transcendentals=0),
    )(part, theirs, inverse, norm)


def shards(n, activations, sketch):
    x, rows = activations, activations.shape[0]
    width = sketch.shape[1]
    depth = n * width
    index = lax.axis_index("tok")
    core = index % 2
    orders = [order for _, order in PIECES]
    sizes = [width * share // 8 for share, _ in PIECES]
    starts = [sum(sizes[:p]) for p in range(len(sizes))]
    every = range(len(PIECES))

    def table(which):
        mine, theirs = [], []
        for order, start in zip(orders, starts):
            owner = jnp.bitwise_xor(index, 2 * jnp.array(owners(order)[which], jnp.int32))
            mine.append((width * owner + start) // 128)
            theirs.append((width * (owner // 2) + start) // 128)
        return jnp.stack(mine + theirs).astype(jnp.int32)

    near, far = table(0), table(1)

    with jax.named_scope("gather_sketch"):
        held = [sketch[0, start : start + size] for start, size in zip(starts, sizes)]
        came = [swap(held[p], 2 * orders[p][0], n) for p in every]
    with jax.named_scope("split_features"):
        x, norm, *others = load(core.reshape(1).astype(jnp.int32), x, width)
        others = lax.optimization_barrier((*others, *came))[:PARTS]
        others = [swap(part, 1, n) for part in others]
    with jax.named_scope("gather_sketch"):
        held = [jnp.concatenate([held[p], came[p]]) for p in every]
        held = [jnp.concatenate([held[p], swap(held[p], 2 * orders[p][1], n)]) for p in every]
        came = [swap(held[p], 2 * orders[p][2], n) for p in every]
    with jax.named_scope("sketched"):
        part = project(near, x, others, held)
        part = project(far, x, others, came, part)
        theirs = swap(part, 1, n)
        sketched = (part + jnp.concatenate([theirs[rows:], theirs[:rows]])).astype(BF16)
    with jax.named_scope("range"):
        sent = spread(far, x, others, sketched, sizes, True)
        kept = spread(near, x, others, sketched, sizes, False)
        sums = []
        for p in every:
            mine, coded = kept[p], sent[p]
            for bit in orders[p][::-1]:
                total = mine + decode(swap(coded, 2 * bit, n))
                cut = total.shape[0] // 2
                mine, coded = total[:cut], encode(total[cut:])
            sums.append(total)
        range_rows = jnp.concatenate(sums, axis=0)
    with jax.named_scope("gram"):
        gram = jnp.dot(range_rows.T, range_rows, preferred_element_type=F32, precision=HIGH)
        grams = [gram]
        for bit in (1, 2, 4, 8):
            gram = gram + swap(gram, bit, n)
            grams.append(gram)
    with jax.named_scope("gather_range"):
        held = [total.astype(BF16) for total in sums]
        held = [jnp.concatenate([held[p], swap(held[p], 2 * orders[p][0], n)]) for p in every]
        held[0] = after(held[0], grams[2])
        held[-1] = after(held[-1], grams[3])
        held = [jnp.concatenate([held[p], swap(held[p], 2 * orders[p][1], n)]) for p in every]
        held[-1] = after(held[-1], grams[4])
        came = [swap(held[p], 2 * orders[p][2], n) for p in every]
    with jax.named_scope("factor"):
        inverse, basis = factored(math.sqrt(depth), gram, range_rows)
    with jax.named_scope("coords"):
        part = project(near, x, others, held)
        part = project(far, x, others, came, after(part, inverse))
        coords, resid_rms = close(depth, part, swap(part[rows:], 1, n), inverse, norm)
    return basis[None], coords, resid_rms.reshape(rows)


def shards_any(depth, activations, sketch):
    sketch_all = lax.all_gather(sketch, "tok", axis=1, tiled=True)[0]
    sketched = lax.psum(jnp.dot(activations, sketch_all, preferred_element_type=F32), "feat").astype(BF16)
    term = lax.dot_general(activations, sketched, (((0,), (0,)), ((), ())), preferred_element_type=F32)
    range_rows = lax.psum_scatter(term, "tok", scatter_dimension=0, tiled=True)
    gram = jnp.dot(range_rows.T, range_rows, preferred_element_type=F32, precision=HIGH)
    factor = jnp.linalg.cholesky(lax.psum(gram, ("tok", "feat")))
    own_rows = jax.scipy.linalg.solve_triangular(factor, range_rows.T, lower=True).T
    half_basis = lax.all_gather(own_rows.astype(BF16), "tok", axis=0, tiled=True)
    basis = (own_rows * F32(math.sqrt(depth)))[None]
    coords = lax.psum(jnp.dot(activations, half_basis, preferred_element_type=F32), "feat")
    rebuilt = jnp.dot(coords.astype(BF16), half_basis.T, preferred_element_type=F32)
    leftover = activations.astype(F32) - rebuilt
    energy = lax.psum(jnp.sum(leftover * leftover, axis=1), "feat")
    return basis, coords, jnp.sqrt(energy / depth + 1e-06)


def solution(mesh):
    n, feat = mesh.shape["tok"], mesh.shape["feat"]

    def call(activations, sketch):
        depth = activations.shape[1]
        if n == 16 and feat == 1:
            body = functools.partial(shards, n)
        else:
            body = functools.partial(shards_any, depth)
        return jax.shard_map(
            body,
            mesh=mesh,
            in_specs=(P(("groups", "tok"), "feat"), P("feat", "tok", None)),
            out_specs=(
                P(("groups", "feat"), "tok", None),
                P(("groups", "tok"), None),
                P(("groups", "tok")),
            ),
            check_vma=False,
        )(activations, sketch)

    return call
```

```python
import functools
import math

import jax
import jax.numpy as jnp
from jax import lax
from jax.experimental import pallas as pl
from jax.experimental.pallas import tpu as pltpu
from jax.sharding import PartitionSpec as P

F32, BF16 = jnp.float32, jnp.bfloat16
HIGH = lax.Precision.HIGHEST
VMEM = pl.BlockSpec(memory_space=pltpu.VMEM)
SMEM = pl.BlockSpec(memory_space=pltpu.SMEM)
ANY = pl.BlockSpec(memory_space=pl.ANY)
PARAMS = pltpu.CompilerParams(vmem_limit_bytes=10 * 2**20)

X_BIT, ZLO, ZHI = 1, 2, 4
HLX, HXL, LHX = (ZHI, ZLO, X_BIT), (ZHI, X_BIT, ZLO), (ZLO, ZHI, X_BIT)
PIECES = ((2, HLX), (2, HXL), (2, HLX), (2, HXL))
LOADS, PARTS = 8, 1
NEAR, FAR = 0, 1


def swap(value, bit, n):
    return lax.ppermute(value, "tok", [(i, i ^ bit) for i in range(n)])


def owners(bits):
    near = [0]
    for bit in bits[:-1]:
        near += [owner ^ bit for owner in near]
    return near, [owner ^ bits[-1] for owner in near]


def layout(width):
    place, out = 0, []
    for share, order in PIECES:
        out.append((place, width * share // 8, owners(order)))
        place += width * share // 8
    return out


def encode(value):
    return (value * jnp.abs(value)).astype(BF16)


def decode(coded):
    wide = coded.astype(F32)
    root = jnp.sqrt(jnp.abs(wide))
    return jnp.where(wide < 0, -root, root)


def after(value, *earlier):
    return lax.optimization_barrier((value, *earlier))[0]


def pinned(value):
    return pltpu.with_memory_space_constraint(value, pltpu.VMEM)


def load_kernel(width, index_ref, x_ref, copy_ref, norm_ref, *refs):
    outs, sems = refs[:-1], refs[-1]
    rows, features = x_ref.shape
    chunk = rows // LOADS

    def copy(i):
        part = pl.ds(i * chunk, chunk)
        return pltpu.make_async_copy(x_ref.at[part, :], copy_ref.at[part, :], sems.at[i])

    for i in range(LOADS):
        copy(i).start()
    for i in range(LOADS):
        copy(i).wait()
        out = outs[i * len(outs) // LOADS]
        base = i * chunk % out.shape[0]
        for k in range(features // (2 * width)):
            start = pl.multiple_of((2 * k + 1 - index_ref[0] % 2) * width, width)
            out[base : base + chunk, k * width : (k + 1) * width] = copy_ref[
                i * chunk : (i + 1) * chunk, pl.ds(start, width)
            ]
        total = jnp.zeros((chunk, 128), F32)
        for k in range(0, features, 128):
            wide = copy_ref[i * chunk : (i + 1) * chunk, k : k + 128].astype(F32)
            total = total + wide * wide
        norm_ref[i * chunk : (i + 1) * chunk, :] = total


def load(index, x, width):
    rows, features = x.shape
    part = (rows // PARTS, features // 2)
    return pl.pallas_call(
        functools.partial(load_kernel, width),
        in_specs=[SMEM, ANY],
        out_specs=[VMEM] * (2 + PARTS),
        out_shape=[pltpu.VMEM(x.shape, BF16), pltpu.VMEM((rows, 128), F32)] + [pltpu.VMEM(part, BF16)] * PARTS,
        scratch_shapes=[pltpu.SemaphoreType.DMA((LOADS,))],
        compiler_params=PARAMS,
        cost_estimate=pl.CostEstimate(flops=2 * rows * features, bytes_accessed=4 * rows * features, transcendentals=0),
    )(index, pltpu.with_memory_space_constraint(x, pltpu.HBM))


def tokens(place, owner, start, size, x_ref, other_refs):
    index_ref, width = place
    block = jnp.bitwise_xor(index_ref[0], 2 * owner)
    mine = x_ref[:, pl.ds(pl.multiple_of(block * width + start, 128), size)]
    where = pl.ds(pl.multiple_of(block // 2 * width + start, 128), size)
    return jnp.concatenate([mine] + [ref[:, where] for ref in other_refs], axis=0)


def project_kernel(width, which, has_init, index_ref, x_ref, *refs):
    others, refs, out_ref = refs[:PARTS], refs[PARTS:-1], refs[-1]
    count = len(PIECES)
    total = refs[count][...] if has_init else None
    for j in range(4):
        left, block = [], []
        for ref, (start, size, lists) in zip(refs, layout(width)):
            left.append(tokens((index_ref, width), lists[which][j], start, size, x_ref, others))
            block.append(ref[j * size : (j + 1) * size, :])
        left, block = jnp.concatenate(left, axis=1), jnp.concatenate(block, axis=0)
        term = jnp.dot(left, block, preferred_element_type=F32)
        total = term if total is None else total + term
    out_ref[...] = total


def project(place, which, x, others, pieces, init=None):
    rows, rank = x.shape[0], pieces[0].shape[1]
    depth = sum(piece.shape[0] for piece in pieces)
    extra = [] if init is None else [init]
    return pl.pallas_call(
        functools.partial(project_kernel, place[1], which, init is not None),
        in_specs=[SMEM] + [VMEM] * (1 + PARTS + len(pieces) + len(extra)),
        out_specs=VMEM,
        out_shape=jax.ShapeDtypeStruct((2 * rows, rank), F32),
        compiler_params=PARAMS,
        cost_estimate=pl.CostEstimate(
            flops=4 * rows * depth * rank, bytes_accessed=4 * rows * depth, transcendentals=0
        ),
    )(place[0], pinned(x), *map(pinned, others), *pieces, *extra)


def spread_kernel(width, which, index_ref, x_ref, *refs):
    others, y_ref, outs = refs[:PARTS], refs[PARTS], refs[PARTS + 1 :]
    turned = y_ref[...].astype(F32).T.astype(BF16)
    for out, (start, size, lists) in zip(outs, layout(width)):
        for j in range(4):
            right = tokens((index_ref, width), lists[which][j], start, size, x_ref, others)
            term = jnp.dot(turned, right, preferred_element_type=F32).T
            out[j * size : (j + 1) * size, :] = encode(term) if which == FAR else term


def spread(place, which, x, others, y):
    rows, rank = x.shape[0], y.shape[1]
    sizes = [size for _, size, _ in layout(place[1])]
    return pl.pallas_call(
        functools.partial(spread_kernel, place[1], which),
        in_specs=[SMEM] + [VMEM] * (2 + PARTS),
        out_specs=[VMEM] * len(sizes),
        out_shape=[jax.ShapeDtypeStruct((4 * size, rank), BF16 if which == FAR else F32) for size in sizes],
        compiler_params=PARAMS,
        cost_estimate=pl.CostEstimate(
            flops=16 * rows * sum(sizes) * rank, bytes_accessed=16 * rows * sum(sizes), transcendentals=0
        ),
    )(place[0], pinned(x), *map(pinned, others), y)


def factor_kernel(scale, gram_ref, range_ref, out_ref, basis_ref):
    n, b = gram_ref.shape[0], 8
    lane = lax.broadcasted_iota(jnp.int32, (b, n), 1)
    sub = lax.broadcasted_iota(jnp.int32, (b, n), 0)

    def full(value):
        return jnp.broadcast_to(value, (b, n))

    tiles = [gram_ref[b * i : b * i + b, :] for i in range(n // b)]
    for t in range(n // b):
        k = b * t
        group = (lane >= k) & (lane < k + b)
        cols = [full(tiles[t][:, k + c : k + c + 1]) for c in range(b)]
        entry = {(r, c): full(cols[c][r : r + 1, :]) for r in range(b) for c in range(r + 1)}
        rows = [jnp.where(lane == k + r, 1.0, jnp.where(group, 0.0, full(tiles[t][r : r + 1, :]))) for r in range(b)]
        invs, low = [], {}
        for c in range(b):
            invs.append(1.0 / entry[c, c])
            for r in range(c + 1, b):
                low[r, c] = entry[r, c] * invs[c]
            for r in range(c + 1, b):
                for s in range(c + 1, r + 1):
                    entry[r, s] = entry[r, s] - low[r, c] * entry[s, c]
            for r in range(c + 1, b):
                rows[r] = rows[r] - low[r, c] * rows[c]
        solved = [row * inv for row, inv in zip(rows, invs)]
        for c in range(b - 1, 0, -1):
            for r in range(c):
                solved[r] = solved[r] - low[c, r] * solved[c]
        for i in range(t + 1, n // b):
            new = jnp.where(group, 0.0, tiles[i])
            for c in range(b):
                new = new - full(tiles[i][:, k + c : k + c + 1]) * solved[c]
            tiles[i] = new
        done, pivots = rows[0], entry[0, 0]
        for r in range(1, b):
            done = jnp.where(sub == r, rows[r], done)
            pivots = jnp.where(sub == r, entry[r, r], pivots)
        out_ref[k : k + b, :] = jnp.where(lane <= k + sub, done, 0.0) * lax.rsqrt(pivots)
    basis_ref[...] = scale * lax.dot_general(
        range_ref[...], out_ref[...], (((1,), (1,)), ((), ())), precision=HIGH, preferred_element_type=F32
    )


def factored(scale, gram, range_rows):
    return pl.pallas_call(
        functools.partial(factor_kernel, scale),
        in_specs=[VMEM] * 2,
        out_specs=[VMEM] * 2,
        out_shape=[jax.ShapeDtypeStruct(gram.shape, F32), jax.ShapeDtypeStruct(range_rows.shape, F32)],
        compiler_params=PARAMS,
        cost_estimate=pl.CostEstimate(flops=10**7, bytes_accessed=2 * 10**7, transcendentals=0),
    )(gram, range_rows)


def close_kernel(depth, part_ref, theirs_ref, inverse_ref, norm_ref, coords_ref, resid_ref):
    raw = part_ref[: theirs_ref.shape[0], :] + theirs_ref[...]
    coords = lax.dot_general(raw, inverse_ref[...], (((1,), (1,)), ((), ())), precision=HIGH)
    coords_ref[...] = coords
    lost = coords - coords.astype(BF16).astype(F32)
    terms = norm_ref[...] + (lost * lost - coords * coords)
    energy = jnp.sum(terms.T, axis=0, keepdims=True)
    resid_ref[...] = jnp.sqrt(jnp.maximum(energy, 0.0) / depth + 1e-06)


def close(depth, part, theirs, inverse, norm):
    rows, rank = theirs.shape
    return pl.pallas_call(
        functools.partial(close_kernel, depth),
        in_specs=[VMEM] * 4,
        out_specs=[VMEM] * 2,
        out_shape=[jax.ShapeDtypeStruct((rows, rank), F32), jax.ShapeDtypeStruct((1, rows), F32)],
        compiler_params=PARAMS,
        cost_estimate=pl.CostEstimate(flops=2 * rows * rank * rank, bytes_accessed=16 * rows * rank, transcendentals=0),
    )(part, theirs, inverse, norm)


def shards(n, activations, sketch):
    x, rows = activations, activations.shape[0]
    width = sketch.shape[1]
    depth = n * width
    index = lax.axis_index("tok").astype(jnp.int32).reshape(1)
    place = (index, width)
    orders = [order for _, order in PIECES]
    every = range(len(PIECES))

    with jax.named_scope("gather_sketch"):
        held = [sketch[0, start : start + size] for start, size, _ in layout(width)]
        came = [swap(held[p], 2 * orders[p][0], n) for p in every]
    with jax.named_scope("split_features"):
        x, norm, *others = load(index, x, width)
        others = lax.optimization_barrier((*others, *came))[:PARTS]
        others = [swap(part, 1, n) for part in others]
    with jax.named_scope("gather_sketch"):
        held = [jnp.concatenate([held[p], came[p]]) for p in every]
        held = [jnp.concatenate([held[p], swap(held[p], 2 * orders[p][1], n)]) for p in every]
        came = [swap(held[p], 2 * orders[p][2], n) for p in every]
    with jax.named_scope("sketched"):
        part = project(place, NEAR, x, others, held)
        part = project(place, FAR, x, others, came, part)
        theirs = swap(part, 1, n)
        sketched = (part + jnp.concatenate([theirs[rows:], theirs[:rows]])).astype(BF16)
    with jax.named_scope("range"):
        sent = spread(place, FAR, x, others, sketched)
        kept = spread(place, NEAR, x, others, sketched)
        sums = []
        for p in every:
            mine, coded = kept[p], sent[p]
            for bit in orders[p][::-1]:
                total = mine + decode(swap(coded, 2 * bit, n))
                cut = total.shape[0] // 2
                mine, coded = total[:cut], encode(total[cut:])
            sums.append(total)
        range_rows = jnp.concatenate(sums, axis=0)
    with jax.named_scope("gram"):
        gram = jnp.dot(range_rows.T, range_rows, preferred_element_type=F32, precision=HIGH)
        grams = [gram]
        for bit in (1, 2):
            gram = gram + swap(gram, bit, n)
            grams.append(gram)
        far = [swap(gram, bit, n) for bit in (4, 8, 12)]
        gram = (gram + far[0]) + (far[1] + far[2])
        grams += [gram, gram]
    with jax.named_scope("gather_range"):
        held = [total.astype(BF16) for total in sums]
        held = [jnp.concatenate([held[p], swap(held[p], 2 * orders[p][0], n)]) for p in every]
        held[0] = after(held[0], grams[2])
        held[-1] = after(held[-1], grams[2])
        held = [jnp.concatenate([held[p], swap(held[p], 2 * orders[p][1], n)]) for p in every]
        came = [swap(held[p], 2 * orders[p][2], n) for p in every]
    with jax.named_scope("factor"):
        inverse, basis = factored(math.sqrt(depth), gram, range_rows)
    with jax.named_scope("coords"):
        part = project(place, NEAR, x, others, held)
        part = project(place, FAR, x, others, came, after(part, inverse))
        coords, resid_rms = close(depth, part, swap(part[rows:], 1, n), inverse, norm)
    return basis[None], coords, resid_rms.reshape(rows)


def shards_any(depth, activations, sketch):
    sketch_all = lax.all_gather(sketch, "tok", axis=1, tiled=True)[0]
    sketched = lax.psum(jnp.dot(activations, sketch_all, preferred_element_type=F32), "feat").astype(BF16)
    term = lax.dot_general(activations, sketched, (((0,), (0,)), ((), ())), preferred_element_type=F32)
    range_rows = lax.psum_scatter(term, "tok", scatter_dimension=0, tiled=True)
    gram = jnp.dot(range_rows.T, range_rows, preferred_element_type=F32, precision=HIGH)
    factor = jnp.linalg.cholesky(lax.psum(gram, ("tok", "feat")))
    own_rows = jax.scipy.linalg.solve_triangular(factor, range_rows.T, lower=True).T
    half_basis = lax.all_gather(own_rows.astype(BF16), "tok", axis=0, tiled=True)
    basis = (own_rows * F32(math.sqrt(depth)))[None]
    coords = lax.psum(jnp.dot(activations, half_basis, preferred_element_type=F32), "feat")
    rebuilt = jnp.dot(coords.astype(BF16), half_basis.T, preferred_element_type=F32)
    leftover = activations.astype(F32) - rebuilt
    energy = lax.psum(jnp.sum(leftover * leftover, axis=1), "feat")
    return basis, coords, jnp.sqrt(energy / depth + 1e-06)


def solution(mesh):
    n, feat = mesh.shape["tok"], mesh.shape["feat"]

    def call(activations, sketch):
        depth = activations.shape[1]
        if n == 16 and feat == 1:
            body = functools.partial(shards, n)
        else:
            body = functools.partial(shards_any, depth)
        return jax.shard_map(
            body,
            mesh=mesh,
            in_specs=(P(("groups", "tok"), "feat"), P("feat", "tok", None)),
            out_specs=(
                P(("groups", "feat"), "tok", None),
                P(("groups", "tok"), None),
                P(("groups", "tok")),
            ),
            check_vma=False,
        )(activations, sketch)

    return call
```

```python
import functools
import math

import jax
import jax.numpy as jnp
from jax import lax
from jax.experimental import pallas as pl
from jax.experimental.pallas import tpu as pltpu
from jax.sharding import PartitionSpec as P

F32, BF16 = jnp.float32, jnp.bfloat16
HIGH = lax.Precision.HIGHEST
VMEM = pl.BlockSpec(memory_space=pltpu.VMEM)
SMEM = pl.BlockSpec(memory_space=pltpu.SMEM)
ANY = pl.BlockSpec(memory_space=pl.ANY)
PARAMS = pltpu.CompilerParams(vmem_limit_bytes=10 * 2**20)

X_BIT, ZLO, ZHI = 1, 2, 4
HLX, HXL, LHX = (ZHI, ZLO, X_BIT), (ZHI, X_BIT, ZLO), (ZLO, ZHI, X_BIT)
SKETCH_PIECES = ((2, HXL, True), (2, HLX, False), (2, HXL, False))
RANGE_PIECES = ((2, HLX, False), (2, HXL, False), (2, LHX, False), (2, HXL, False))
LOADS, PARTS = 8, 1
TIED = 2


def swap(value, bit, n):
    return lax.ppermute(value, "tok", [(i, i ^ bit) for i in range(n)])


def owners(bits):
    near = [0]
    for bit in bits[:-1]:
        near += [owner ^ bit for owner in near]
    return near, [owner ^ bits[-1] for owner in near]


def layout(width, pieces):
    place, out = 0, []
    for share, order, shared in pieces:
        size = width * share // 8
        out.append((place, size, owners(order)))
        place += size * (2 if shared else 1)
    return out


def encode(value):
    return (value * jnp.abs(value)).astype(BF16)


def decode(coded):
    wide = coded.astype(F32)
    root = jnp.sqrt(jnp.abs(wide))
    return jnp.where(wide < 0, -root, root)


def after(value, *earlier):
    return lax.optimization_barrier((value, *earlier))[0]


def pinned(value):
    return pltpu.with_memory_space_constraint(value, pltpu.VMEM)


def load_kernel(width, index_ref, x_ref, copy_ref, norm_ref, *refs):
    outs, sems = refs[:-1], refs[-1]
    rows, features = x_ref.shape
    chunk = rows // LOADS

    def copy(i):
        part = pl.ds(i * chunk, chunk)
        return pltpu.make_async_copy(x_ref.at[part, :], copy_ref.at[part, :], sems.at[i])

    for i in range(LOADS):
        copy(i).start()
    for i in range(LOADS):
        copy(i).wait()
        out = outs[i * len(outs) // LOADS]
        base = i * chunk % out.shape[0]
        for k in range(features // (2 * width)):
            start = pl.multiple_of((2 * k + 1 - index_ref[0] % 2) * width, width)
            out[base : base + chunk, k * width : (k + 1) * width] = copy_ref[
                i * chunk : (i + 1) * chunk, pl.ds(start, width)
            ]
        total = jnp.zeros((chunk, 128), F32)
        for k in range(0, features, 128):
            wide = copy_ref[i * chunk : (i + 1) * chunk, k : k + 128].astype(F32)
            total = total + wide * wide
        norm_ref[i * chunk : (i + 1) * chunk, :] = total


def load(index, x, width):
    rows, features = x.shape
    part = (rows // PARTS, features // 2)
    return pl.pallas_call(
        functools.partial(load_kernel, width),
        in_specs=[SMEM, ANY],
        out_specs=[VMEM] * (2 + PARTS),
        out_shape=[pltpu.VMEM(x.shape, BF16), pltpu.VMEM((rows, 128), F32)] + [pltpu.VMEM(part, BF16)] * PARTS,
        scratch_shapes=[pltpu.SemaphoreType.DMA((LOADS,))],
        compiler_params=PARAMS,
        cost_estimate=pl.CostEstimate(flops=2 * rows * features, bytes_accessed=4 * rows * features, transcendentals=0),
    )(index, pltpu.with_memory_space_constraint(x, pltpu.HBM))


def tokens(index_ref, group_ref, width, entry, j, x_ref, other_refs):
    owner, start, size, flip = entry
    block = jnp.bitwise_xor(index_ref[0], 2 * owner[j])
    if flip is not None:
        start = start + jnp.bitwise_xor(group_ref[0], flip) * size
    mine = x_ref[:, pl.ds(pl.multiple_of(block * width + start, 128), size)]
    where = pl.ds(pl.multiple_of(block // 2 * width + start, 128), size)
    return jnp.concatenate([mine] + [ref[:, where] for ref in other_refs], axis=0)


def project_kernel(width, entries, has_init, index_ref, group_ref, x_ref, *refs):
    others, refs, out_ref = refs[:PARTS], refs[PARTS:-1], refs[-1]
    total = refs[len(entries)][...] if has_init else None
    for j in range(4):
        left = [tokens(index_ref, group_ref, width, entry, j, x_ref, others) for entry in entries]
        block = [ref[j * entry[2] : (j + 1) * entry[2], :] for ref, entry in zip(refs, entries)]
        term = jnp.dot(
            jnp.concatenate(left, axis=1), jnp.concatenate(block, axis=0), preferred_element_type=F32
        )
        total = term if total is None else total + term
    out_ref[...] = total


def project(place, entries, x, others, arrays, init=None):
    index, group, width = place
    rows, rank = x.shape[0], arrays[0].shape[1]
    depth = sum(array.shape[0] for array in arrays)
    extra = [] if init is None else [init]
    return pl.pallas_call(
        functools.partial(project_kernel, width, entries, init is not None),
        in_specs=[SMEM] * 2 + [VMEM] * (1 + PARTS + len(arrays) + len(extra)),
        out_specs=VMEM,
        out_shape=jax.ShapeDtypeStruct((2 * rows, rank), F32),
        compiler_params=PARAMS,
        cost_estimate=pl.CostEstimate(
            flops=4 * rows * depth * rank, bytes_accessed=4 * rows * depth, transcendentals=0
        ),
    )(index, group, pinned(x), *map(pinned, others), *arrays, *extra)


def spread_kernel(width, entries, coded, index_ref, group_ref, x_ref, *refs):
    others, y_ref, outs = refs[:PARTS], refs[PARTS], refs[PARTS + 1 :]
    turned = y_ref[...].astype(F32).T.astype(BF16)
    for out, entry in zip(outs, entries):
        size = entry[2]
        for j in range(4):
            right = tokens(index_ref, group_ref, width, entry, j, x_ref, others)
            term = jnp.dot(turned, right, preferred_element_type=F32).T
            out[j * size : (j + 1) * size, :] = encode(term) if coded else term


def spread(place, entries, coded, x, others, y):
    index, group, width = place
    rows, rank = x.shape[0], y.shape[1]
    sizes = [entry[2] for entry in entries]
    return pl.pallas_call(
        functools.partial(spread_kernel, width, entries, coded),
        in_specs=[SMEM] * 2 + [VMEM] * (2 + PARTS),
        out_specs=[VMEM] * len(sizes),
        out_shape=[jax.ShapeDtypeStruct((4 * size, rank), BF16 if coded else F32) for size in sizes],
        compiler_params=PARAMS,
        cost_estimate=pl.CostEstimate(
            flops=16 * rows * sum(sizes) * rank, bytes_accessed=16 * rows * sum(sizes), transcendentals=0
        ),
    )(index, group, pinned(x), *map(pinned, others), y)


def factor_kernel(scale, gram_ref, range_ref, out_ref, basis_ref):
    n, b = gram_ref.shape[0], 8
    lane = lax.broadcasted_iota(jnp.int32, (b, n), 1)
    sub = lax.broadcasted_iota(jnp.int32, (b, n), 0)

    def full(value):
        return jnp.broadcast_to(value, (b, n))

    tiles = [gram_ref[b * i : b * i + b, :] for i in range(n // b)]
    for t in range(n // b):
        k = b * t
        group = (lane >= k) & (lane < k + b)
        cols = [full(tiles[t][:, k + c : k + c + 1]) for c in range(b)]
        entry = {(r, c): full(cols[c][r : r + 1, :]) for r in range(b) for c in range(r + 1)}
        rows = [jnp.where(lane == k + r, 1.0, jnp.where(group, 0.0, full(tiles[t][r : r + 1, :]))) for r in range(b)]
        invs, low = [], {}
        for c in range(b):
            invs.append(1.0 / entry[c, c])
            for r in range(c + 1, b):
                low[r, c] = entry[r, c] * invs[c]
            for r in range(c + 1, b):
                for s in range(c + 1, r + 1):
                    entry[r, s] = entry[r, s] - low[r, c] * entry[s, c]
            for r in range(c + 1, b):
                rows[r] = rows[r] - low[r, c] * rows[c]
        solved = [row * inv for row, inv in zip(rows, invs)]
        for c in range(b - 1, 0, -1):
            for r in range(c):
                solved[r] = solved[r] - low[c, r] * solved[c]
        for i in range(t + 1, n // b):
            new = jnp.where(group, 0.0, tiles[i])
            for c in range(b):
                new = new - full(tiles[i][:, k + c : k + c + 1]) * solved[c]
            tiles[i] = new
        done, pivots = rows[0], entry[0, 0]
        for r in range(1, b):
            done = jnp.where(sub == r, rows[r], done)
            pivots = jnp.where(sub == r, entry[r, r], pivots)
        out_ref[k : k + b, :] = jnp.where(lane <= k + sub, done, 0.0) * lax.rsqrt(pivots)
    basis_ref[...] = scale * lax.dot_general(
        range_ref[...], out_ref[...], (((1,), (1,)), ((), ())), precision=HIGH, preferred_element_type=F32
    )


def factored(scale, gram, range_rows):
    return pl.pallas_call(
        functools.partial(factor_kernel, scale),
        in_specs=[VMEM] * 2,
        out_specs=[VMEM] * 2,
        out_shape=[jax.ShapeDtypeStruct(gram.shape, F32), jax.ShapeDtypeStruct(range_rows.shape, F32)],
        compiler_params=PARAMS,
        cost_estimate=pl.CostEstimate(flops=10**7, bytes_accessed=2 * 10**7, transcendentals=0),
    )(gram, range_rows)


def close_kernel(depth, part_ref, theirs_ref, inverse_ref, norm_ref, coords_ref, resid_ref):
    raw = part_ref[: theirs_ref.shape[0], :] + theirs_ref[...]
    coords = lax.dot_general(raw, inverse_ref[...], (((1,), (1,)), ((), ())), precision=HIGH)
    coords_ref[...] = coords
    lost = coords - coords.astype(BF16).astype(F32)
    terms = norm_ref[...] + (lost * lost - coords * coords)
    energy = jnp.sum(terms.T, axis=0, keepdims=True)
    resid_ref[...] = jnp.sqrt(jnp.maximum(energy, 0.0) / depth + 1e-06)


def close(depth, part, theirs, inverse, norm):
    rows, rank = theirs.shape
    return pl.pallas_call(
        functools.partial(close_kernel, depth),
        in_specs=[VMEM] * 4,
        out_specs=[VMEM] * 2,
        out_shape=[jax.ShapeDtypeStruct((rows, rank), F32), jax.ShapeDtypeStruct((1, rows), F32)],
        compiler_params=PARAMS,
        cost_estimate=pl.CostEstimate(flops=2 * rows * rank * rank, bytes_accessed=16 * rows * rank, transcendentals=0),
    )(part, theirs, inverse, norm)


def shards(n, activations, sketch):
    x, rows = activations, activations.shape[0]
    width, rank = sketch.shape[1:]
    depth = n * width
    index, group = (lax.axis_index(axis).astype(jnp.int32).reshape(1) for axis in ("tok", "groups"))
    place = (index, group, width)

    def across(value):
        return lax.ppermute(value, "groups", [(0, 1), (1, 0)])

    with jax.named_scope("gather_sketch"):
        pieces = layout(width, SKETCH_PIECES)
        held = []
        for (start, size, _), (_, _, shared) in zip(pieces, SKETCH_PIECES):
            first = start + (group[0] * size if shared else 0)
            held.append(lax.dynamic_slice(sketch[0], (first, 0), (size, rank)))
        came = [swap(held[p], 2 * order[0], n) for p, (_, order, _) in enumerate(SKETCH_PIECES)]
    with jax.named_scope("split_features"):
        x, norm, *others = load(index, x, width)
        others = lax.optimization_barrier((*others, *came[:TIED]))[:PARTS]
        others = [swap(part, 1, n) for part in others]
    with jax.named_scope("gather_sketch"):
        near, near_rows, far, far_rows = [], [], [], []
        for p, (share, order, shared) in enumerate(SKETCH_PIECES):
            start, size, (near_owners, far_owners) = pieces[p]
            own = 0 if shared else None
            first = jnp.concatenate([held[p], came[p]])
            array = jnp.concatenate([first, swap(first, 2 * order[1], n)])
            last = swap(array, 2 * order[2], n)
            near.append(array)
            near_rows.append((near_owners, start, size, own))
            far.append(last)
            far_rows.append((far_owners, start, size, own))
            if shared:
                far += [across(array), across(last)]
                far_rows += [(near_owners, start, size, 1), (far_owners, start, size, 1)]
    with jax.named_scope("sketched"):
        part = project(place, near_rows, x, others, near)
        part = project(place, far_rows, x, others, far, part)
        theirs = swap(part, 1, n)
        sketched = (part + jnp.concatenate([theirs[rows:], theirs[:rows]])).astype(BF16)
    with jax.named_scope("range"):
        orders = [order for _, order, _ in RANGE_PIECES]
        every = range(len(orders))
        pieces = layout(width, RANGE_PIECES)
        near_rows = [(near_owners, start, size, None) for start, size, (near_owners, _) in pieces]
        far_rows = [(far_owners, start, size, None) for start, size, (_, far_owners) in pieces]
        sent = spread(place, far_rows, True, x, others, sketched)
        kept = spread(place, near_rows, False, x, others, sketched)
        sums, held = [], []
        for p in every:
            mine, coded = kept[p], sent[p]
            for bit in orders[p][:0:-1]:
                total = mine + decode(swap(coded, 2 * bit, n))
                cut = total.shape[0] // 2
                mine, coded = total[:cut], encode(total[cut:])
            theirs = decode(swap(encode(total), 2 * orders[p][0], n))
            own = total[:cut] + theirs[cut:]
            sums.append(own)
            held.append(jnp.concatenate([own, total[cut:] + theirs[:cut]]).astype(BF16))
        range_rows = jnp.concatenate(sums, axis=0)
    with jax.named_scope("gram"):
        gram = jnp.dot(range_rows.T, range_rows, preferred_element_type=F32, precision=HIGH)
        for bit in (1, 2):
            gram = gram + swap(gram, bit, n)
        apart = [swap(gram, bit, n) for bit in (4, 8, 12)]
        gram = (gram + apart[0]) + (apart[1] + apart[2])
    with jax.named_scope("gather_range"):
        held = [jnp.concatenate([held[p], swap(held[p], 2 * orders[p][1], n)]) for p in every]
        came = [swap(held[p], 2 * orders[p][2], n) for p in every]
    with jax.named_scope("factor"):
        inverse, basis = factored(math.sqrt(depth), gram, range_rows)
    with jax.named_scope("coords"):
        part = project(place, near_rows, x, others, held)
        part = project(place, far_rows, x, others, came, after(part, inverse))
        coords, resid_rms = close(depth, part, swap(part[rows:], 1, n), inverse, norm)
    return basis[None], coords, resid_rms.reshape(rows)


def shards_any(depth, activations, sketch):
    sketch_all = lax.all_gather(sketch, "tok", axis=1, tiled=True)[0]
    sketched = lax.psum(jnp.dot(activations, sketch_all, preferred_element_type=F32), "feat").astype(BF16)
    term = lax.dot_general(activations, sketched, (((0,), (0,)), ((), ())), preferred_element_type=F32)
    range_rows = lax.psum_scatter(term, "tok", scatter_dimension=0, tiled=True)
    gram = jnp.dot(range_rows.T, range_rows, preferred_element_type=F32, precision=HIGH)
    factor = jnp.linalg.cholesky(lax.psum(gram, ("tok", "feat")))
    own_rows = jax.scipy.linalg.solve_triangular(factor, range_rows.T, lower=True).T
    half_basis = lax.all_gather(own_rows.astype(BF16), "tok", axis=0, tiled=True)
    basis = (own_rows * F32(math.sqrt(depth)))[None]
    coords = lax.psum(jnp.dot(activations, half_basis, preferred_element_type=F32), "feat")
    rebuilt = jnp.dot(coords.astype(BF16), half_basis.T, preferred_element_type=F32)
    leftover = activations.astype(F32) - rebuilt
    energy = lax.psum(jnp.sum(leftover * leftover, axis=1), "feat")
    return basis, coords, jnp.sqrt(energy / depth + 1e-06)


def solution(mesh):
    n, feat = mesh.shape["tok"], mesh.shape["feat"]

    def call(activations, sketch):
        depth = activations.shape[1]
        if n == 16 and feat == 1:
            body = functools.partial(shards, n)
        else:
            body = functools.partial(shards_any, depth)
        return jax.shard_map(
            body,
            mesh=mesh,
            in_specs=(P(("groups", "tok"), "feat"), P("feat", "tok", None)),
            out_specs=(
                P(("groups", "feat"), "tok", None),
                P(("groups", "tok"), None),
                P(("groups", "tok")),
            ),
            check_vma=False,
        )(activations, sketch)

    return call
```

```python
import functools
import math

import jax
import jax.numpy as jnp
from jax import lax
from jax.experimental import pallas as pl
from jax.experimental.pallas import tpu as pltpu
from jax.sharding import PartitionSpec as P

F32, BF16 = jnp.float32, jnp.bfloat16
HIGH = lax.Precision.HIGHEST
VMEM = pl.BlockSpec(memory_space=pltpu.VMEM)
SMEM = pl.BlockSpec(memory_space=pltpu.SMEM)
ANY = pl.BlockSpec(memory_space=pl.ANY)
PARAMS = pltpu.CompilerParams(vmem_limit_bytes=10 * 2**20)

X_BIT, ZLO, ZHI = 1, 2, 4
HLX, HXL, LHX = (ZHI, ZLO, X_BIT), (ZHI, X_BIT, ZLO), (ZLO, ZHI, X_BIT)
SKETCH_PIECES = ((2, HXL, True), (2, HLX, False), (2, HXL, False))
RANGE_PIECES = ((2, HLX, False), (2, HXL, False), (2, LHX, False), (2, HXL, False))
LOADS, PARTS = 8, 1
TIED = 2


def swap(value, bit, n):
    return lax.ppermute(value, "tok", [(i, i ^ bit) for i in range(n)])


def owners(bits):
    near = [0]
    for bit in bits[:-1]:
        near += [owner ^ bit for owner in near]
    return near, [owner ^ bits[-1] for owner in near]


def layout(width, pieces):
    place, out = 0, []
    for share, order, shared in pieces:
        size = width * share // 8
        out.append((place, size, owners(order)))
        place += size * (2 if shared else 1)
    return out


def encode(value):
    return (value * jnp.abs(value)).astype(BF16)


def decode(coded):
    wide = coded.astype(F32)
    root = jnp.sqrt(jnp.abs(wide))
    return jnp.where(wide < 0, -root, root)


def after(value, *earlier):
    return lax.optimization_barrier((value, *earlier))[0]


def pinned(value):
    return pltpu.with_memory_space_constraint(value, pltpu.VMEM)


def load_kernel(width, index_ref, x_ref, copy_ref, norm_ref, *refs):
    outs, sems = refs[:-1], refs[-1]
    rows, features = x_ref.shape
    chunk = rows // LOADS

    def copy(i):
        part = pl.ds(i * chunk, chunk)
        return pltpu.make_async_copy(x_ref.at[part, :], copy_ref.at[part, :], sems.at[i])

    for i in range(LOADS):
        copy(i).start()
    for i in range(LOADS):
        copy(i).wait()
        out = outs[i * len(outs) // LOADS]
        base = i * chunk % out.shape[0]
        for k in range(features // (2 * width)):
            start = pl.multiple_of((2 * k + 1 - index_ref[0] % 2) * width, width)
            out[base : base + chunk, k * width : (k + 1) * width] = copy_ref[
                i * chunk : (i + 1) * chunk, pl.ds(start, width)
            ]
        total = jnp.zeros((chunk, 128), F32)
        for k in range(0, features, 128):
            wide = copy_ref[i * chunk : (i + 1) * chunk, k : k + 128].astype(F32)
            total = total + wide * wide
        norm_ref[i * chunk : (i + 1) * chunk, :] = total


def load(index, x, width):
    rows, features = x.shape
    part = (rows // PARTS, features // 2)
    return pl.pallas_call(
        functools.partial(load_kernel, width),
        in_specs=[SMEM, ANY],
        out_specs=[VMEM] * (2 + PARTS),
        out_shape=[pltpu.VMEM(x.shape, BF16), pltpu.VMEM((rows, 128), F32)] + [pltpu.VMEM(part, BF16)] * PARTS,
        scratch_shapes=[pltpu.SemaphoreType.DMA((LOADS,))],
        compiler_params=PARAMS,
        cost_estimate=pl.CostEstimate(flops=2 * rows * features, bytes_accessed=4 * rows * features, transcendentals=0),
    )(index, pltpu.with_memory_space_constraint(x, pltpu.HBM))


def tokens(index_ref, group_ref, width, entry, j, x_ref, other_refs):
    owner, start, size, flip = entry
    block = jnp.bitwise_xor(index_ref[0], 2 * owner[j])
    if flip is not None:
        start = start + jnp.bitwise_xor(group_ref[0], flip) * size
    mine = x_ref[:, pl.ds(pl.multiple_of(block * width + start, 128), size)]
    where = pl.ds(pl.multiple_of(block // 2 * width + start, 128), size)
    return jnp.concatenate([mine] + [ref[:, where] for ref in other_refs], axis=0)


def project_kernel(width, entries, has_init, index_ref, group_ref, x_ref, *refs):
    others, refs, out_ref = refs[:PARTS], refs[PARTS:-1], refs[-1]
    total = refs[len(entries)][...] if has_init else None
    for j in range(4):
        left = [tokens(index_ref, group_ref, width, entry, j, x_ref, others) for entry in entries]
        block = [ref[j * entry[2] : (j + 1) * entry[2], :] for ref, entry in zip(refs, entries)]
        term = jnp.dot(
            jnp.concatenate(left, axis=1), jnp.concatenate(block, axis=0), preferred_element_type=F32
        )
        total = term if total is None else total + term
    out_ref[...] = total


def project(place, entries, x, others, arrays, init=None):
    index, group, width = place
    rows, rank = x.shape[0], arrays[0].shape[1]
    depth = sum(array.shape[0] for array in arrays)
    extra = [] if init is None else [init]
    return pl.pallas_call(
        functools.partial(project_kernel, width, entries, init is not None),
        in_specs=[SMEM] * 2 + [VMEM] * (1 + PARTS + len(arrays) + len(extra)),
        out_specs=VMEM,
        out_shape=jax.ShapeDtypeStruct((2 * rows, rank), F32),
        compiler_params=PARAMS,
        cost_estimate=pl.CostEstimate(
            flops=4 * rows * depth * rank, bytes_accessed=4 * rows * depth, transcendentals=0
        ),
    )(index, group, pinned(x), *map(pinned, others), *arrays, *extra)


def spread_kernel(width, entries, coded, index_ref, group_ref, x_ref, *refs):
    others, y_ref, outs = refs[:PARTS], refs[PARTS], refs[PARTS + 1 :]
    turned = y_ref[...].astype(F32).T.astype(BF16)
    for out, entry in zip(outs, entries):
        size = entry[2]
        for j in range(4):
            right = tokens(index_ref, group_ref, width, entry, j, x_ref, others)
            term = jnp.dot(turned, right, preferred_element_type=F32).T
            out[j * size : (j + 1) * size, :] = encode(term) if coded else term


def spread(place, entries, coded, x, others, y):
    index, group, width = place
    rows, rank = x.shape[0], y.shape[1]
    sizes = [entry[2] for entry in entries]
    return pl.pallas_call(
        functools.partial(spread_kernel, width, entries, coded),
        in_specs=[SMEM] * 2 + [VMEM] * (2 + PARTS),
        out_specs=[VMEM] * len(sizes),
        out_shape=[jax.ShapeDtypeStruct((4 * size, rank), BF16 if coded else F32) for size in sizes],
        compiler_params=PARAMS,
        cost_estimate=pl.CostEstimate(
            flops=16 * rows * sum(sizes) * rank, bytes_accessed=16 * rows * sum(sizes), transcendentals=0
        ),
    )(index, group, pinned(x), *map(pinned, others), y)


def factor_kernel(scale, gram_ref, range_ref, out_ref, basis_ref):
    n, b = gram_ref.shape[0], 8
    lane = lax.broadcasted_iota(jnp.int32, (b, n), 1)
    sub = lax.broadcasted_iota(jnp.int32, (b, n), 0)

    def full(value):
        return jnp.broadcast_to(value, (b, n))

    tiles = [gram_ref[b * i : b * i + b, :] for i in range(n // b)]
    for t in range(n // b):
        k = b * t
        group = (lane >= k) & (lane < k + b)
        cols = [full(tiles[t][:, k + c : k + c + 1]) for c in range(b)]
        entry = {(r, c): full(cols[c][r : r + 1, :]) for r in range(b) for c in range(r + 1)}
        rows = [jnp.where(lane == k + r, 1.0, jnp.where(group, 0.0, full(tiles[t][r : r + 1, :]))) for r in range(b)]
        invs, low = [], {}
        for c in range(b):
            invs.append(1.0 / entry[c, c])
            for r in range(c + 1, b):
                low[r, c] = entry[r, c] * invs[c]
            for r in range(c + 1, b):
                for s in range(c + 1, r + 1):
                    entry[r, s] = entry[r, s] - low[r, c] * entry[s, c]
            for r in range(c + 1, b):
                rows[r] = rows[r] - low[r, c] * rows[c]
        solved = [row * inv for row, inv in zip(rows, invs)]
        for c in range(b - 1, 0, -1):
            for r in range(c):
                solved[r] = solved[r] - low[c, r] * solved[c]
        for i in range(t + 1, n // b):
            new = jnp.where(group, 0.0, tiles[i])
            for c in range(b):
                new = new - full(tiles[i][:, k + c : k + c + 1]) * solved[c]
            tiles[i] = new
        done, pivots = rows[0], entry[0, 0]
        for r in range(1, b):
            done = jnp.where(sub == r, rows[r], done)
            pivots = jnp.where(sub == r, entry[r, r], pivots)
        out_ref[k : k + b, :] = jnp.where(lane <= k + sub, done, 0.0) * lax.rsqrt(pivots)
    basis_ref[...] = scale * lax.dot_general(
        range_ref[...], out_ref[...], (((1,), (1,)), ((), ())), precision=HIGH, preferred_element_type=F32
    )


def factored(scale, gram, range_rows):
    return pl.pallas_call(
        functools.partial(factor_kernel, scale),
        in_specs=[VMEM] * 2,
        out_specs=[VMEM] * 2,
        out_shape=[jax.ShapeDtypeStruct(gram.shape, F32), jax.ShapeDtypeStruct(range_rows.shape, F32)],
        compiler_params=PARAMS,
        cost_estimate=pl.CostEstimate(flops=10**7, bytes_accessed=2 * 10**7, transcendentals=0),
    )(gram, range_rows)


def close_kernel(depth, part_ref, theirs_ref, inverse_ref, norm_ref, coords_ref, resid_ref):
    raw = part_ref[: theirs_ref.shape[0], :] + theirs_ref[...]
    coords = lax.dot_general(raw, inverse_ref[...], (((1,), (1,)), ((), ())), precision=HIGH)
    coords_ref[...] = coords
    lost = coords - coords.astype(BF16).astype(F32)
    terms = norm_ref[...] + (lost * lost - coords * coords)
    energy = jnp.sum(terms.T, axis=0, keepdims=True)
    resid_ref[...] = jnp.sqrt(jnp.maximum(energy, 0.0) / depth + 1e-06)


def close(depth, part, theirs, inverse, norm):
    rows, rank = theirs.shape
    return pl.pallas_call(
        functools.partial(close_kernel, depth),
        in_specs=[VMEM] * 4,
        out_specs=[VMEM] * 2,
        out_shape=[jax.ShapeDtypeStruct((rows, rank), F32), jax.ShapeDtypeStruct((1, rows), F32)],
        compiler_params=PARAMS,
        cost_estimate=pl.CostEstimate(flops=2 * rows * rank * rank, bytes_accessed=16 * rows * rank, transcendentals=0),
    )(part, theirs, inverse, norm)


def shards(n, activations, sketch):
    x, rows = activations, activations.shape[0]
    width, rank = sketch.shape[1:]
    depth = n * width
    index, group = (lax.axis_index(axis).astype(jnp.int32).reshape(1) for axis in ("tok", "groups"))
    place = (index, group, width)

    def across(value):
        return lax.ppermute(value, "groups", [(0, 1), (1, 0)])

    with jax.named_scope("gather_sketch"):
        pieces = layout(width, SKETCH_PIECES)
        held = []
        for (start, size, _), (_, _, shared) in zip(pieces, SKETCH_PIECES):
            first = start + (group[0] * size if shared else 0)
            held.append(lax.dynamic_slice(sketch[0], (first, 0), (size, rank)))
        came = [swap(held[p], 2 * order[0], n) for p, (_, order, _) in enumerate(SKETCH_PIECES)]
    with jax.named_scope("split_features"):
        x, norm, *others = load(index, x, width)
        others = lax.optimization_barrier((*others, *came[:TIED]))[:PARTS]
        others = [swap(part, 1, n) for part in others]
    with jax.named_scope("gather_sketch"):
        near, near_rows, far, far_rows = [], [], [], []
        for p, (share, order, shared) in enumerate(SKETCH_PIECES):
            start, size, (near_owners, far_owners) = pieces[p]
            own = 0 if shared else None
            first = jnp.concatenate([held[p], came[p]])
            array = jnp.concatenate([first, swap(first, 2 * order[1], n)])
            last = swap(array, 2 * order[2], n)
            near.append(array)
            near_rows.append((near_owners, start, size, own))
            far.append(last)
            far_rows.append((far_owners, start, size, own))
            if shared:
                far += [across(array), across(last)]
                far_rows += [(near_owners, start, size, 1), (far_owners, start, size, 1)]
    with jax.named_scope("sketched"):
        part = project(place, near_rows, x, others, near)
        part = project(place, far_rows, x, others, far, part)
        theirs = swap(part, 1, n)
        sketched = (part + jnp.concatenate([theirs[rows:], theirs[:rows]])).astype(BF16)
    with jax.named_scope("range"):
        orders = [order for _, order, _ in RANGE_PIECES]
        every = range(len(orders))
        pieces = layout(width, RANGE_PIECES)
        near_rows = [(near_owners, start, size, None) for start, size, (near_owners, _) in pieces]
        far_rows = [(far_owners, start, size, None) for start, size, (_, far_owners) in pieces]
        sent = spread(place, far_rows, True, x, others, sketched)
        kept = spread(place, near_rows, False, x, others, sketched)
        sums, held = [], []
        for p in every:
            mine, coded = kept[p], sent[p]
            for bit in orders[p][:0:-1]:
                total = mine + decode(swap(coded, 2 * bit, n))
                cut = total.shape[0] // 2
                mine, coded = total[:cut], encode(total[cut:])
            theirs = decode(swap(encode(total), 2 * orders[p][0], n))
            own = total[:cut] + theirs[cut:]
            sums.append(own)
            held.append(jnp.concatenate([own, total[cut:] + theirs[:cut]]).astype(BF16))
        range_rows = jnp.concatenate(sums, axis=0)
    with jax.named_scope("gather_range"):
        came = [swap(held[p], 2 * orders[p][1], n) for p in every]
    with jax.named_scope("gram"):
        gram = jnp.dot(range_rows.T, range_rows, preferred_element_type=F32, precision=HIGH)
        for bit in (1, 2):
            gram = gram + swap(gram, bit, n)
        gram = after(gram, came[1])
        apart = [swap(gram, bit, n) for bit in (4, 8, 12)]
        gram = (gram + apart[0]) + (apart[1] + apart[2])
    with jax.named_scope("gather_range"):
        held = [jnp.concatenate([held[p], came[p]]) for p in every]
        came = [swap(held[p], 2 * orders[p][2], n) for p in every]
    with jax.named_scope("factor"):
        inverse, basis = factored(math.sqrt(depth), gram, range_rows)
    with jax.named_scope("coords"):
        part = project(place, near_rows, x, others, held)
        part = project(place, far_rows, x, others, came, after(part, inverse))
        coords, resid_rms = close(depth, part, swap(part[rows:], 1, n), inverse, norm)
    return basis[None], coords, resid_rms.reshape(rows)


def shards_any(depth, activations, sketch):
    sketch_all = lax.all_gather(sketch, "tok", axis=1, tiled=True)[0]
    sketched = lax.psum(jnp.dot(activations, sketch_all, preferred_element_type=F32), "feat").astype(BF16)
    term = lax.dot_general(activations, sketched, (((0,), (0,)), ((), ())), preferred_element_type=F32)
    range_rows = lax.psum_scatter(term, "tok", scatter_dimension=0, tiled=True)
    gram = jnp.dot(range_rows.T, range_rows, preferred_element_type=F32, precision=HIGH)
    factor = jnp.linalg.cholesky(lax.psum(gram, ("tok", "feat")))
    own_rows = jax.scipy.linalg.solve_triangular(factor, range_rows.T, lower=True).T
    half_basis = lax.all_gather(own_rows.astype(BF16), "tok", axis=0, tiled=True)
    basis = (own_rows * F32(math.sqrt(depth)))[None]
    coords = lax.psum(jnp.dot(activations, half_basis, preferred_element_type=F32), "feat")
    rebuilt = jnp.dot(coords.astype(BF16), half_basis.T, preferred_element_type=F32)
    leftover = activations.astype(F32) - rebuilt
    energy = lax.psum(jnp.sum(leftover * leftover, axis=1), "feat")
    return basis, coords, jnp.sqrt(energy / depth + 1e-06)


def solution(mesh):
    n, feat = mesh.shape["tok"], mesh.shape["feat"]

    def call(activations, sketch):
        depth = activations.shape[1]
        if n == 16 and feat == 1:
            body = functools.partial(shards, n)
        else:
            body = functools.partial(shards_any, depth)
        return jax.shard_map(
            body,
            mesh=mesh,
            in_specs=(P(("groups", "tok"), "feat"), P("feat", "tok", None)),
            out_specs=(
                P(("groups", "feat"), "tok", None),
                P(("groups", "tok"), None),
                P(("groups", "tok")),
            ),
            check_vma=False,
        )(activations, sketch)

    return call
```

```python
import functools
import math

import jax
import jax.numpy as jnp
from jax import lax
from jax.experimental import pallas as pl
from jax.experimental.pallas import tpu as pltpu
from jax.sharding import PartitionSpec as P

F32, BF16 = jnp.float32, jnp.bfloat16
HIGH = lax.Precision.HIGHEST
VMEM = pl.BlockSpec(memory_space=pltpu.VMEM)
SMEM = pl.BlockSpec(memory_space=pltpu.SMEM)
ANY = pl.BlockSpec(memory_space=pl.ANY)
PARAMS = pltpu.CompilerParams(vmem_limit_bytes=10 * 2**20)

X_BIT, ZLO, ZHI = 1, 2, 4
HLX, HXL, LHX = (ZHI, ZLO, X_BIT), (ZHI, X_BIT, ZLO), (ZLO, ZHI, X_BIT)
SKETCH_PIECES = ((2, HXL, True), (2, HLX, False), (2, HXL, False))
RANGE_PIECES = ((2, HXL, False), (2, HLX, False), (2, LHX, False), (2, HXL, False))
LOADS, PARTS = 8, 1
TIED = 2


def swap(value, bit, n):
    return lax.ppermute(value, "tok", [(i, i ^ bit) for i in range(n)])


def owners(bits):
    near = [0]
    for bit in bits[:-1]:
        near += [owner ^ bit for owner in near]
    return near, [owner ^ bits[-1] for owner in near]


def layout(width, pieces):
    place, out = 0, []
    for share, order, shared in pieces:
        size = width * share // 8
        out.append((place, size, owners(order)))
        place += size * (2 if shared else 1)
    return out


def encode(value):
    return (value * jnp.abs(value)).astype(BF16)


def decode(coded):
    wide = coded.astype(F32)
    root = jnp.sqrt(jnp.abs(wide))
    return jnp.where(wide < 0, -root, root)


def after(value, *earlier):
    return lax.optimization_barrier((value, *earlier))[0]


def pinned(value):
    return pltpu.with_memory_space_constraint(value, pltpu.VMEM)


def load_kernel(width, index_ref, x_ref, copy_ref, norm_ref, *refs):
    outs, sems = refs[:-1], refs[-1]
    rows, features = x_ref.shape
    chunk = rows // LOADS

    def copy(i):
        part = pl.ds(i * chunk, chunk)
        return pltpu.make_async_copy(x_ref.at[part, :], copy_ref.at[part, :], sems.at[i])

    for i in range(LOADS):
        copy(i).start()
    for i in range(LOADS):
        copy(i).wait()
        out = outs[i * len(outs) // LOADS]
        base = i * chunk % out.shape[0]
        for k in range(features // (2 * width)):
            start = pl.multiple_of((2 * k + 1 - index_ref[0] % 2) * width, width)
            out[base : base + chunk, k * width : (k + 1) * width] = copy_ref[
                i * chunk : (i + 1) * chunk, pl.ds(start, width)
            ]
        total = jnp.zeros((chunk, 128), F32)
        for k in range(0, features, 128):
            wide = copy_ref[i * chunk : (i + 1) * chunk, k : k + 128].astype(F32)
            total = total + wide * wide
        norm_ref[i * chunk : (i + 1) * chunk, :] = total


def load(index, x, width):
    rows, features = x.shape
    part = (rows // PARTS, features // 2)
    return pl.pallas_call(
        functools.partial(load_kernel, width),
        in_specs=[SMEM, ANY],
        out_specs=[VMEM] * (2 + PARTS),
        out_shape=[pltpu.VMEM(x.shape, BF16), pltpu.VMEM((rows, 128), F32)] + [pltpu.VMEM(part, BF16)] * PARTS,
        scratch_shapes=[pltpu.SemaphoreType.DMA((LOADS,))],
        compiler_params=PARAMS,
        cost_estimate=pl.CostEstimate(flops=2 * rows * features, bytes_accessed=4 * rows * features, transcendentals=0),
    )(index, pltpu.with_memory_space_constraint(x, pltpu.HBM))


def tokens(index_ref, group_ref, width, entry, j, x_ref, other_refs):
    owner, start, size, flip = entry
    block = jnp.bitwise_xor(index_ref[0], 2 * owner[j])
    if flip is not None:
        start = start + jnp.bitwise_xor(group_ref[0], flip) * size
    mine = x_ref[:, pl.ds(pl.multiple_of(block * width + start, 128), size)]
    where = pl.ds(pl.multiple_of(block // 2 * width + start, 128), size)
    return jnp.concatenate([mine] + [ref[:, where] for ref in other_refs], axis=0)


def project_kernel(width, entries, has_init, index_ref, group_ref, x_ref, *refs):
    others, refs, out_ref = refs[:PARTS], refs[PARTS:-1], refs[-1]
    total = refs[len(entries)][...] if has_init else None
    for j in range(4):
        left = [tokens(index_ref, group_ref, width, entry, j, x_ref, others) for entry in entries]
        block = [ref[j * entry[2] : (j + 1) * entry[2], :] for ref, entry in zip(refs, entries)]
        term = jnp.dot(
            jnp.concatenate(left, axis=1), jnp.concatenate(block, axis=0), preferred_element_type=F32
        )
        total = term if total is None else total + term
    out_ref[...] = total


def project(place, entries, x, others, arrays, init=None):
    index, group, width = place
    rows, rank = x.shape[0], arrays[0].shape[1]
    depth = sum(array.shape[0] for array in arrays)
    extra = [] if init is None else [init]
    return pl.pallas_call(
        functools.partial(project_kernel, width, entries, init is not None),
        in_specs=[SMEM] * 2 + [VMEM] * (1 + PARTS + len(arrays) + len(extra)),
        out_specs=VMEM,
        out_shape=jax.ShapeDtypeStruct((2 * rows, rank), F32),
        compiler_params=PARAMS,
        cost_estimate=pl.CostEstimate(
            flops=4 * rows * depth * rank, bytes_accessed=4 * rows * depth, transcendentals=0
        ),
    )(index, group, pinned(x), *map(pinned, others), *arrays, *extra)


def spread_kernel(width, entries, coded, index_ref, group_ref, x_ref, *refs):
    others, y_ref, outs = refs[:PARTS], refs[PARTS], refs[PARTS + 1 :]
    turned = y_ref[...].astype(F32).T.astype(BF16)
    for out, entry in zip(outs, entries):
        size = entry[2]
        for j in range(4):
            right = tokens(index_ref, group_ref, width, entry, j, x_ref, others)
            term = jnp.dot(turned, right, preferred_element_type=F32).T
            out[j * size : (j + 1) * size, :] = encode(term) if coded else term


def spread(place, entries, coded, x, others, y):
    index, group, width = place
    rows, rank = x.shape[0], y.shape[1]
    sizes = [entry[2] for entry in entries]
    return pl.pallas_call(
        functools.partial(spread_kernel, width, entries, coded),
        in_specs=[SMEM] * 2 + [VMEM] * (2 + PARTS),
        out_specs=[VMEM] * len(sizes),
        out_shape=[jax.ShapeDtypeStruct((4 * size, rank), BF16 if coded else F32) for size in sizes],
        compiler_params=PARAMS,
        cost_estimate=pl.CostEstimate(
            flops=16 * rows * sum(sizes) * rank, bytes_accessed=16 * rows * sum(sizes), transcendentals=0
        ),
    )(index, group, pinned(x), *map(pinned, others), y)


def factor_kernel(scale, gram_ref, range_ref, out_ref, basis_ref):
    n, b = gram_ref.shape[0], 8
    lane = lax.broadcasted_iota(jnp.int32, (b, n), 1)
    sub = lax.broadcasted_iota(jnp.int32, (b, n), 0)

    def full(value):
        return jnp.broadcast_to(value, (b, n))

    tiles = [gram_ref[b * i : b * i + b, :] for i in range(n // b)]
    for t in range(n // b):
        k = b * t
        group = (lane >= k) & (lane < k + b)
        cols = [full(tiles[t][:, k + c : k + c + 1]) for c in range(b)]
        entry = {(r, c): full(cols[c][r : r + 1, :]) for r in range(b) for c in range(r + 1)}
        rows = [jnp.where(lane == k + r, 1.0, jnp.where(group, 0.0, full(tiles[t][r : r + 1, :]))) for r in range(b)]
        invs, low = [], {}
        for c in range(b):
            invs.append(1.0 / entry[c, c])
            for r in range(c + 1, b):
                low[r, c] = entry[r, c] * invs[c]
            for r in range(c + 1, b):
                for s in range(c + 1, r + 1):
                    entry[r, s] = entry[r, s] - low[r, c] * entry[s, c]
            for r in range(c + 1, b):
                rows[r] = rows[r] - low[r, c] * rows[c]
        solved = [row * inv for row, inv in zip(rows, invs)]
        for c in range(b - 1, 0, -1):
            for r in range(c):
                solved[r] = solved[r] - low[c, r] * solved[c]
        for i in range(t + 1, n // b):
            new = jnp.where(group, 0.0, tiles[i])
            for c in range(b):
                new = new - full(tiles[i][:, k + c : k + c + 1]) * solved[c]
            tiles[i] = new
        done, pivots = rows[0], entry[0, 0]
        for r in range(1, b):
            done = jnp.where(sub == r, rows[r], done)
            pivots = jnp.where(sub == r, entry[r, r], pivots)
        out_ref[k : k + b, :] = jnp.where(lane <= k + sub, done, 0.0) * lax.rsqrt(pivots)
    basis_ref[...] = scale * lax.dot_general(
        range_ref[...], out_ref[...], (((1,), (1,)), ((), ())), precision=HIGH, preferred_element_type=F32
    )


def factored(scale, gram, range_rows):
    return pl.pallas_call(
        functools.partial(factor_kernel, scale),
        in_specs=[VMEM] * 2,
        out_specs=[VMEM] * 2,
        out_shape=[jax.ShapeDtypeStruct(gram.shape, F32), jax.ShapeDtypeStruct(range_rows.shape, F32)],
        compiler_params=PARAMS,
        cost_estimate=pl.CostEstimate(flops=10**7, bytes_accessed=2 * 10**7, transcendentals=0),
    )(gram, range_rows)


def close_kernel(depth, part_ref, theirs_ref, inverse_ref, norm_ref, coords_ref, resid_ref):
    raw = part_ref[: theirs_ref.shape[0], :] + theirs_ref[...]
    coords = lax.dot_general(raw, inverse_ref[...], (((1,), (1,)), ((), ())), precision=HIGH)
    coords_ref[...] = coords
    lost = coords - coords.astype(BF16).astype(F32)
    terms = norm_ref[...] + (lost * lost - coords * coords)
    energy = jnp.sum(terms.T, axis=0, keepdims=True)
    resid_ref[...] = jnp.sqrt(jnp.maximum(energy, 0.0) / depth + 1e-06)


def close(depth, part, theirs, inverse, norm):
    rows, rank = theirs.shape
    return pl.pallas_call(
        functools.partial(close_kernel, depth),
        in_specs=[VMEM] * 4,
        out_specs=[VMEM] * 2,
        out_shape=[jax.ShapeDtypeStruct((rows, rank), F32), jax.ShapeDtypeStruct((1, rows), F32)],
        compiler_params=PARAMS,
        cost_estimate=pl.CostEstimate(flops=2 * rows * rank * rank, bytes_accessed=16 * rows * rank, transcendentals=0),
    )(part, theirs, inverse, norm)


def shards(n, activations, sketch):
    x, rows = activations, activations.shape[0]
    width, rank = sketch.shape[1:]
    depth = n * width
    index, group = (lax.axis_index(axis).astype(jnp.int32).reshape(1) for axis in ("tok", "groups"))
    place = (index, group, width)

    def across(value):
        return lax.ppermute(value, "groups", [(0, 1), (1, 0)])

    with jax.named_scope("gather_sketch"):
        pieces = layout(width, SKETCH_PIECES)
        held = []
        for (start, size, _), (_, _, shared) in zip(pieces, SKETCH_PIECES):
            first = start + (group[0] * size if shared else 0)
            held.append(lax.dynamic_slice(sketch[0], (first, 0), (size, rank)))
        came = [swap(held[p], 2 * order[0], n) for p, (_, order, _) in enumerate(SKETCH_PIECES)]
    with jax.named_scope("split_features"):
        x, norm, *others = load(index, x, width)
        others = lax.optimization_barrier((*others, *came[:TIED]))[:PARTS]
        others = [swap(part, 1, n) for part in others]
    with jax.named_scope("gather_sketch"):
        near, near_rows, far, far_rows = [], [], [], []
        for p, (share, order, shared) in enumerate(SKETCH_PIECES):
            start, size, (near_owners, far_owners) = pieces[p]
            own = 0 if shared else None
            first = jnp.concatenate([held[p], came[p]])
            array = jnp.concatenate([first, swap(first, 2 * order[1], n)])
            last = swap(array, 2 * order[2], n)
            near.append(array)
            near_rows.append((near_owners, start, size, own))
            far.append(last)
            far_rows.append((far_owners, start, size, own))
            if shared:
                far += [across(array), across(last)]
                far_rows += [(near_owners, start, size, 1), (far_owners, start, size, 1)]
    with jax.named_scope("sketched"):
        part = project(place, near_rows, x, others, near)
        part = project(place, far_rows, x, others, far, part)
        theirs = swap(part, 1, n)
        sketched = (part + jnp.concatenate([theirs[rows:], theirs[:rows]])).astype(BF16)
    with jax.named_scope("range"):
        orders = [order for _, order, _ in RANGE_PIECES]
        every = range(len(orders))
        pieces = layout(width, RANGE_PIECES)
        near_rows = [(near_owners, start, size, None) for start, size, (near_owners, _) in pieces]
        far_rows = [(far_owners, start, size, None) for start, size, (_, far_owners) in pieces]
        sent = spread(place, far_rows, True, x, others, sketched)
        kept = spread(place, near_rows, False, x, others, sketched)
        sums, held = [], []
        for p in every:
            mine, coded = kept[p], sent[p]
            for bit in orders[p][:0:-1]:
                total = mine + decode(swap(coded, 2 * bit, n))
                cut = total.shape[0] // 2
                mine, coded = total[:cut], encode(total[cut:])
            theirs = decode(swap(encode(total), 2 * orders[p][0], n))
            own = total[:cut] + theirs[cut:]
            sums.append(own)
            held.append(jnp.concatenate([own, total[cut:] + theirs[:cut]]).astype(BF16))
        range_rows = jnp.concatenate(sums, axis=0)
    with jax.named_scope("gather_range"):
        came = [swap(held[p], 2 * orders[p][1], n) for p in every]
    with jax.named_scope("gram"):
        gram = jnp.dot(range_rows.T, range_rows, preferred_element_type=F32, precision=HIGH)
        for bit in (1, 2):
            gram = gram + swap(gram, bit, n)
        gram = after(gram, came[0])
        apart = [swap(gram, bit, n) for bit in (4, 8, 12)]
        gram = (gram + apart[0]) + (apart[1] + apart[2])
    with jax.named_scope("gather_range"):
        held = [jnp.concatenate([held[p], came[p]]) for p in every]
        came = [swap(held[p], 2 * orders[p][2], n) for p in every]
    with jax.named_scope("factor"):
        inverse, basis = factored(math.sqrt(depth), gram, range_rows)
    with jax.named_scope("coords"):
        part = project(place, near_rows, x, others, held)
        part = project(place, far_rows, x, others, came, after(part, inverse))
        coords, resid_rms = close(depth, part, swap(part[rows:], 1, n), inverse, norm)
    return basis[None], coords, resid_rms.reshape(rows)


def shards_any(depth, activations, sketch):
    sketch_all = lax.all_gather(sketch, "tok", axis=1, tiled=True)[0]
    sketched = lax.psum(jnp.dot(activations, sketch_all, preferred_element_type=F32), "feat").astype(BF16)
    term = lax.dot_general(activations, sketched, (((0,), (0,)), ((), ())), preferred_element_type=F32)
    range_rows = lax.psum_scatter(term, "tok", scatter_dimension=0, tiled=True)
    gram = jnp.dot(range_rows.T, range_rows, preferred_element_type=F32, precision=HIGH)
    factor = jnp.linalg.cholesky(lax.psum(gram, ("tok", "feat")))
    own_rows = jax.scipy.linalg.solve_triangular(factor, range_rows.T, lower=True).T
    half_basis = lax.all_gather(own_rows.astype(BF16), "tok", axis=0, tiled=True)
    basis = (own_rows * F32(math.sqrt(depth)))[None]
    coords = lax.psum(jnp.dot(activations, half_basis, preferred_element_type=F32), "feat")
    rebuilt = jnp.dot(coords.astype(BF16), half_basis.T, preferred_element_type=F32)
    leftover = activations.astype(F32) - rebuilt
    energy = lax.psum(jnp.sum(leftover * leftover, axis=1), "feat")
    return basis, coords, jnp.sqrt(energy / depth + 1e-06)


def solution(mesh):
    n, feat = mesh.shape["tok"], mesh.shape["feat"]

    def call(activations, sketch):
        depth = activations.shape[1]
        if n == 16 and feat == 1:
            body = functools.partial(shards, n)
        else:
            body = functools.partial(shards_any, depth)
        return jax.shard_map(
            body,
            mesh=mesh,
            in_specs=(P(("groups", "tok"), "feat"), P("feat", "tok", None)),
            out_specs=(
                P(("groups", "feat"), "tok", None),
                P(("groups", "tok"), None),
                P(("groups", "tok")),
            ),
            check_vma=False,
        )(activations, sketch)

    return call
```

```python
import functools
import math

import jax
import jax.numpy as jnp
from jax import lax
from jax.experimental import pallas as pl
from jax.experimental.pallas import tpu as pltpu
from jax.sharding import PartitionSpec as P

F32, BF16 = jnp.float32, jnp.bfloat16
HIGH = lax.Precision.HIGHEST
VMEM = pl.BlockSpec(memory_space=pltpu.VMEM)
SMEM = pl.BlockSpec(memory_space=pltpu.SMEM)
ANY = pl.BlockSpec(memory_space=pl.ANY)
PARAMS = pltpu.CompilerParams(vmem_limit_bytes=10 * 2**20)

X_BIT, ZLO, ZHI = 1, 2, 4
HLX, HXL, LHX = (ZHI, ZLO, X_BIT), (ZHI, X_BIT, ZLO), (ZLO, ZHI, X_BIT)
SKETCH_PIECES = ((2, HXL, True), (2, HLX, False), (2, HXL, False))
RANGE_PIECES = ((2, HXL, False), (2, HLX, False), (2, LHX, False), (2, HXL, False))
LOADS, PARTS = 8, 1
TIED = 2
LAST = 2


def swap(value, bit, n):
    return lax.ppermute(value, "tok", [(i, i ^ bit) for i in range(n)])


def owners(bits):
    near = [0]
    for bit in bits[:-1]:
        near += [owner ^ bit for owner in near]
    return near, [owner ^ bits[-1] for owner in near]


def layout(width, pieces):
    place, out = 0, []
    for share, order, shared in pieces:
        size = width * share // 8
        out.append((place, size, owners(order)))
        place += size * (2 if shared else 1)
    return out


def encode(value):
    return (value * jnp.abs(value)).astype(BF16)


def decode(coded):
    wide = coded.astype(F32)
    root = jnp.sqrt(jnp.abs(wide))
    return jnp.where(wide < 0, -root, root)


def after(value, *earlier):
    return lax.optimization_barrier((value, *earlier))[0]


def pinned(value):
    return pltpu.with_memory_space_constraint(value, pltpu.VMEM)


def load_kernel(width, index_ref, x_ref, copy_ref, norm_ref, *refs):
    outs, sems = refs[:-1], refs[-1]
    rows, features = x_ref.shape
    chunk = rows // LOADS

    def copy(i):
        part = pl.ds(i * chunk, chunk)
        return pltpu.make_async_copy(x_ref.at[part, :], copy_ref.at[part, :], sems.at[i])

    for i in range(LOADS):
        copy(i).start()
    for i in range(LOADS):
        copy(i).wait()
        out = outs[i * len(outs) // LOADS]
        base = i * chunk % out.shape[0]
        for k in range(features // (2 * width)):
            start = pl.multiple_of((2 * k + 1 - index_ref[0] % 2) * width, width)
            out[base : base + chunk, k * width : (k + 1) * width] = copy_ref[
                i * chunk : (i + 1) * chunk, pl.ds(start, width)
            ]
        total = jnp.zeros((chunk, 128), F32)
        for k in range(0, features, 128):
            wide = copy_ref[i * chunk : (i + 1) * chunk, k : k + 128].astype(F32)
            total = total + wide * wide
        norm_ref[i * chunk : (i + 1) * chunk, :] = total


def load(index, x, width):
    rows, features = x.shape
    part = (rows // PARTS, features // 2)
    return pl.pallas_call(
        functools.partial(load_kernel, width),
        in_specs=[SMEM, ANY],
        out_specs=[VMEM] * (2 + PARTS),
        out_shape=[pltpu.VMEM(x.shape, BF16), pltpu.VMEM((rows, 128), F32)] + [pltpu.VMEM(part, BF16)] * PARTS,
        scratch_shapes=[pltpu.SemaphoreType.DMA((LOADS,))],
        compiler_params=PARAMS,
        cost_estimate=pl.CostEstimate(flops=2 * rows * features, bytes_accessed=4 * rows * features, transcendentals=0),
    )(index, pltpu.with_memory_space_constraint(x, pltpu.HBM))


def tokens(index_ref, group_ref, width, entry, j, x_ref, other_refs):
    owner, start, size, flip = entry
    block = jnp.bitwise_xor(index_ref[0], 2 * owner[j])
    if flip is not None:
        start = start + jnp.bitwise_xor(group_ref[0], flip) * size
    mine = x_ref[:, pl.ds(pl.multiple_of(block * width + start, 128), size)]
    where = pl.ds(pl.multiple_of(block // 2 * width + start, 128), size)
    return jnp.concatenate([mine] + [ref[:, where] for ref in other_refs], axis=0)


def project_kernel(width, entries, has_init, index_ref, group_ref, x_ref, *refs):
    others, refs, out_ref = refs[:PARTS], refs[PARTS:-1], refs[-1]
    total = refs[len(entries)][...] if has_init else None
    for j in range(4):
        left = [tokens(index_ref, group_ref, width, entry, j, x_ref, others) for entry in entries]
        block = [ref[j * entry[2] : (j + 1) * entry[2], :] for ref, entry in zip(refs, entries)]
        term = jnp.dot(
            jnp.concatenate(left, axis=1), jnp.concatenate(block, axis=0), preferred_element_type=F32
        )
        total = term if total is None else total + term
    out_ref[...] = total


def project(place, entries, x, others, arrays, init=None):
    index, group, width = place
    rows, rank = x.shape[0], arrays[0].shape[1]
    depth = sum(array.shape[0] for array in arrays)
    extra = [] if init is None else [init]
    return pl.pallas_call(
        functools.partial(project_kernel, width, entries, init is not None),
        in_specs=[SMEM] * 2 + [VMEM] * (1 + PARTS + len(arrays) + len(extra)),
        out_specs=VMEM,
        out_shape=jax.ShapeDtypeStruct((2 * rows, rank), F32),
        compiler_params=PARAMS,
        cost_estimate=pl.CostEstimate(
            flops=4 * rows * depth * rank, bytes_accessed=4 * rows * depth, transcendentals=0
        ),
    )(index, group, pinned(x), *map(pinned, others), *arrays, *extra)


def spread_kernel(width, entries, coded, index_ref, group_ref, x_ref, *refs):
    others, y_ref, outs = refs[:PARTS], refs[PARTS], refs[PARTS + 1 :]
    turned = y_ref[...].astype(F32).T.astype(BF16)
    for out, entry in zip(outs, entries):
        size = entry[2]
        for j in range(4):
            right = tokens(index_ref, group_ref, width, entry, j, x_ref, others)
            term = jnp.dot(turned, right, preferred_element_type=F32).T
            out[j * size : (j + 1) * size, :] = encode(term) if coded else term


def spread(place, entries, coded, x, others, y):
    index, group, width = place
    rows, rank = x.shape[0], y.shape[1]
    sizes = [entry[2] for entry in entries]
    return pl.pallas_call(
        functools.partial(spread_kernel, width, entries, coded),
        in_specs=[SMEM] * 2 + [VMEM] * (2 + PARTS),
        out_specs=[VMEM] * len(sizes),
        out_shape=[jax.ShapeDtypeStruct((4 * size, rank), BF16 if coded else F32) for size in sizes],
        compiler_params=PARAMS,
        cost_estimate=pl.CostEstimate(
            flops=16 * rows * sum(sizes) * rank, bytes_accessed=16 * rows * sum(sizes), transcendentals=0
        ),
    )(index, group, pinned(x), *map(pinned, others), y)


def factor_kernel(scale, gram_ref, range_ref, out_ref, basis_ref):
    n, b = gram_ref.shape[0], 8
    lane = lax.broadcasted_iota(jnp.int32, (b, n), 1)
    sub = lax.broadcasted_iota(jnp.int32, (b, n), 0)

    def full(value):
        return jnp.broadcast_to(value, (b, n))

    tiles = [gram_ref[b * i : b * i + b, :] for i in range(n // b)]
    for t in range(n // b):
        k = b * t
        group = (lane >= k) & (lane < k + b)
        cols = [full(tiles[t][:, k + c : k + c + 1]) for c in range(b)]
        entry = {(r, c): full(cols[c][r : r + 1, :]) for r in range(b) for c in range(r + 1)}
        rows = [jnp.where(lane == k + r, 1.0, jnp.where(group, 0.0, full(tiles[t][r : r + 1, :]))) for r in range(b)]
        invs, low = [], {}
        for c in range(b):
            invs.append(1.0 / entry[c, c])
            for r in range(c + 1, b):
                low[r, c] = entry[r, c] * invs[c]
            for r in range(c + 1, b):
                for s in range(c + 1, r + 1):
                    entry[r, s] = entry[r, s] - low[r, c] * entry[s, c]
            for r in range(c + 1, b):
                rows[r] = rows[r] - low[r, c] * rows[c]
        solved = [row * inv for row, inv in zip(rows, invs)]
        for c in range(b - 1, 0, -1):
            for r in range(c):
                solved[r] = solved[r] - low[c, r] * solved[c]
        for i in range(t + 1, n // b):
            new = jnp.where(group, 0.0, tiles[i])
            for c in range(b):
                new = new - full(tiles[i][:, k + c : k + c + 1]) * solved[c]
            tiles[i] = new
        done, pivots = rows[0], entry[0, 0]
        for r in range(1, b):
            done = jnp.where(sub == r, rows[r], done)
            pivots = jnp.where(sub == r, entry[r, r], pivots)
        out_ref[k : k + b, :] = jnp.where(lane <= k + sub, done, 0.0) * lax.rsqrt(pivots)
    basis_ref[...] = scale * lax.dot_general(
        range_ref[...], out_ref[...], (((1,), (1,)), ((), ())), precision=HIGH, preferred_element_type=F32
    )


def factored(scale, gram, range_rows):
    return pl.pallas_call(
        functools.partial(factor_kernel, scale),
        in_specs=[VMEM] * 2,
        out_specs=[VMEM] * 2,
        out_shape=[jax.ShapeDtypeStruct(gram.shape, F32), jax.ShapeDtypeStruct(range_rows.shape, F32)],
        compiler_params=PARAMS,
        cost_estimate=pl.CostEstimate(flops=10**7, bytes_accessed=2 * 10**7, transcendentals=0),
    )(gram, range_rows)


def close_kernel(depth, part_ref, theirs_ref, inverse_ref, norm_ref, coords_ref, resid_ref):
    raw = part_ref[: theirs_ref.shape[0], :] + theirs_ref[...]
    coords = lax.dot_general(raw, inverse_ref[...], (((1,), (1,)), ((), ())), precision=HIGH)
    coords_ref[...] = coords
    lost = coords - coords.astype(BF16).astype(F32)
    terms = norm_ref[...] + (lost * lost - coords * coords)
    energy = jnp.sum(terms.T, axis=0, keepdims=True)
    resid_ref[...] = jnp.sqrt(jnp.maximum(energy, 0.0) / depth + 1e-06)


def close(depth, part, theirs, inverse, norm):
    rows, rank = theirs.shape
    return pl.pallas_call(
        functools.partial(close_kernel, depth),
        in_specs=[VMEM] * 4,
        out_specs=[VMEM] * 2,
        out_shape=[jax.ShapeDtypeStruct((rows, rank), F32), jax.ShapeDtypeStruct((1, rows), F32)],
        compiler_params=PARAMS,
        cost_estimate=pl.CostEstimate(flops=2 * rows * rank * rank, bytes_accessed=16 * rows * rank, transcendentals=0),
    )(part, theirs, inverse, norm)


def shards(n, activations, sketch):
    x, rows = activations, activations.shape[0]
    width, rank = sketch.shape[1:]
    depth = n * width
    index, group = (lax.axis_index(axis).astype(jnp.int32).reshape(1) for axis in ("tok", "groups"))
    place = (index, group, width)

    def across(value):
        return lax.ppermute(value, "groups", [(0, 1), (1, 0)])

    with jax.named_scope("gather_sketch"):
        pieces = layout(width, SKETCH_PIECES)
        held = []
        for (start, size, _), (_, _, shared) in zip(pieces, SKETCH_PIECES):
            first = start + (group[0] * size if shared else 0)
            held.append(lax.dynamic_slice(sketch[0], (first, 0), (size, rank)))
        came = [swap(held[p], 2 * order[0], n) for p, (_, order, _) in enumerate(SKETCH_PIECES)]
    with jax.named_scope("split_features"):
        x, norm, *others = load(index, x, width)
        others = lax.optimization_barrier((*others, *came[:TIED]))[:PARTS]
        others = [swap(part, 1, n) for part in others]
    with jax.named_scope("gather_sketch"):
        near, near_rows, far, far_rows = [], [], [], []
        for p, (share, order, shared) in enumerate(SKETCH_PIECES):
            start, size, (near_owners, far_owners) = pieces[p]
            own = 0 if shared else None
            first = jnp.concatenate([held[p], came[p]])
            array = jnp.concatenate([first, swap(first, 2 * order[1], n)])
            last = swap(array, 2 * order[2], n)
            near.append(array)
            near_rows.append((near_owners, start, size, own))
            far.append(last)
            far_rows.append((far_owners, start, size, own))
            if shared:
                far += [across(array), across(last)]
                far_rows += [(near_owners, start, size, 1), (far_owners, start, size, 1)]
    with jax.named_scope("sketched"):
        part = project(place, near_rows, x, others, near)
        early = [i for i in range(len(far)) if i != LAST]
        part = project(place, [far_rows[i] for i in early], x, others, [far[i] for i in early], part)
        part = project(place, far_rows[LAST : LAST + 1], x, others, far[LAST : LAST + 1], part)
        theirs = swap(part, 1, n)
        sketched = (part + jnp.concatenate([theirs[rows:], theirs[:rows]])).astype(BF16)
    with jax.named_scope("range"):
        orders = [order for _, order, _ in RANGE_PIECES]
        every = range(len(orders))
        pieces = layout(width, RANGE_PIECES)
        near_rows = [(near_owners, start, size, None) for start, size, (near_owners, _) in pieces]
        far_rows = [(far_owners, start, size, None) for start, size, (_, far_owners) in pieces]
        sent = spread(place, far_rows, True, x, others, sketched)
        kept = spread(place, near_rows, False, x, others, sketched)
        sums, held = [], []
        for p in every:
            mine, coded = kept[p], sent[p]
            for bit in orders[p][:0:-1]:
                total = mine + decode(swap(coded, 2 * bit, n))
                cut = total.shape[0] // 2
                mine, coded = total[:cut], encode(total[cut:])
            theirs = decode(swap(encode(total), 2 * orders[p][0], n))
            own = total[:cut] + theirs[cut:]
            sums.append(own)
            held.append(jnp.concatenate([own, total[cut:] + theirs[:cut]]).astype(BF16))
        range_rows = jnp.concatenate(sums, axis=0)
    with jax.named_scope("gather_range"):
        came = [swap(held[p], 2 * orders[p][1], n) for p in every]
    with jax.named_scope("gram"):
        gram = jnp.dot(range_rows.T, range_rows, preferred_element_type=F32, precision=HIGH)
        for bit in (1, 2):
            gram = gram + swap(gram, bit, n)
        gram = after(gram, came[0])
        apart = [swap(gram, bit, n) for bit in (4, 8, 12)]
        gram = (gram + apart[0]) + (apart[1] + apart[2])
    with jax.named_scope("gather_range"):
        held = [jnp.concatenate([held[p], came[p]]) for p in every]
        came = [swap(held[p], 2 * orders[p][2], n) for p in every]
    with jax.named_scope("factor"):
        inverse, basis = factored(math.sqrt(depth), gram, range_rows)
    with jax.named_scope("coords"):
        part = project(place, near_rows, x, others, held)
        part = project(place, far_rows[:-1], x, others, came[:-1], after(part, inverse))
        part = project(place, far_rows[-1:], x, others, came[-1:], part)
        coords, resid_rms = close(depth, part, swap(part[rows:], 1, n), inverse, norm)
    return basis[None], coords, resid_rms.reshape(rows)


def shards_any(depth, activations, sketch):
    sketch_all = lax.all_gather(sketch, "tok", axis=1, tiled=True)[0]
    sketched = lax.psum(jnp.dot(activations, sketch_all, preferred_element_type=F32), "feat").astype(BF16)
    term = lax.dot_general(activations, sketched, (((0,), (0,)), ((), ())), preferred_element_type=F32)
    range_rows = lax.psum_scatter(term, "tok", scatter_dimension=0, tiled=True)
    gram = jnp.dot(range_rows.T, range_rows, preferred_element_type=F32, precision=HIGH)
    factor = jnp.linalg.cholesky(lax.psum(gram, ("tok", "feat")))
    own_rows = jax.scipy.linalg.solve_triangular(factor, range_rows.T, lower=True).T
    half_basis = lax.all_gather(own_rows.astype(BF16), "tok", axis=0, tiled=True)
    basis = (own_rows * F32(math.sqrt(depth)))[None]
    coords = lax.psum(jnp.dot(activations, half_basis, preferred_element_type=F32), "feat")
    rebuilt = jnp.dot(coords.astype(BF16), half_basis.T, preferred_element_type=F32)
    leftover = activations.astype(F32) - rebuilt
    energy = lax.psum(jnp.sum(leftover * leftover, axis=1), "feat")
    return basis, coords, jnp.sqrt(energy / depth + 1e-06)


def solution(mesh):
    n, feat = mesh.shape["tok"], mesh.shape["feat"]

    def call(activations, sketch):
        depth = activations.shape[1]
        if n == 16 and feat == 1:
            body = functools.partial(shards, n)
        else:
            body = functools.partial(shards_any, depth)
        return jax.shard_map(
            body,
            mesh=mesh,
            in_specs=(P(("groups", "tok"), "feat"), P("feat", "tok", None)),
            out_specs=(
                P(("groups", "feat"), "tok", None),
                P(("groups", "tok"), None),
                P(("groups", "tok")),
            ),
            check_vma=False,
        )(activations, sketch)

    return call
```

```python
import functools
import math

import jax
import jax.numpy as jnp
from jax import lax
from jax.experimental import pallas as pl
from jax.experimental.pallas import tpu as pltpu
from jax.sharding import PartitionSpec as P

F32, BF16 = jnp.float32, jnp.bfloat16
HIGH = lax.Precision.HIGHEST
VMEM = pl.BlockSpec(memory_space=pltpu.VMEM)
SMEM = pl.BlockSpec(memory_space=pltpu.SMEM)
ANY = pl.BlockSpec(memory_space=pl.ANY)
PARAMS = pltpu.CompilerParams(vmem_limit_bytes=10 * 2**20)

X_BIT, ZLO, ZHI = 1, 2, 4
HLX, HXL, LHX = (ZHI, ZLO, X_BIT), (ZHI, X_BIT, ZLO), (ZLO, ZHI, X_BIT)
SKETCH_PIECES = ((2, HXL, True), (2, HLX, False), (2, HXL, False))
RANGE_PIECES = ((2, HXL, False), (2, HLX, False), (2, LHX, False), (2, HXL, False))
LOADS, PARTS = 8, 1
TIED = 2
LAST = 2


def swap(value, bit, n):
    return lax.ppermute(value, "tok", [(i, i ^ bit) for i in range(n)])


def owners(bits):
    near = [0]
    for bit in bits[:-1]:
        near += [owner ^ bit for owner in near]
    return near, [owner ^ bits[-1] for owner in near]


def layout(width, pieces):
    place, out = 0, []
    for share, order, shared in pieces:
        size = width * share // 8
        out.append((place, size, owners(order)))
        place += size * (2 if shared else 1)
    return out


def encode(value):
    return (value * jnp.abs(value)).astype(BF16)


def decode(coded):
    wide = coded.astype(F32)
    root = jnp.sqrt(jnp.abs(wide))
    return jnp.where(wide < 0, -root, root)


def after(value, *earlier):
    return lax.optimization_barrier((value, *earlier))[0]


def pinned(value):
    return pltpu.with_memory_space_constraint(value, pltpu.VMEM)


def load_kernel(width, index_ref, x_ref, copy_ref, norm_ref, *refs):
    outs, sems = refs[:-1], refs[-1]
    rows, features = x_ref.shape
    chunk = rows // LOADS

    def copy(i):
        part = pl.ds(i * chunk, chunk)
        return pltpu.make_async_copy(x_ref.at[part, :], copy_ref.at[part, :], sems.at[i])

    for i in range(LOADS):
        copy(i).start()
    for i in range(LOADS):
        copy(i).wait()
        out = outs[i * len(outs) // LOADS]
        base = i * chunk % out.shape[0]
        for k in range(features // (2 * width)):
            start = pl.multiple_of((2 * k + 1 - index_ref[0] % 2) * width, width)
            out[base : base + chunk, k * width : (k + 1) * width] = copy_ref[
                i * chunk : (i + 1) * chunk, pl.ds(start, width)
            ]
        total = jnp.zeros((chunk, 128), F32)
        for k in range(0, features, 128):
            wide = copy_ref[i * chunk : (i + 1) * chunk, k : k + 128].astype(F32)
            total = total + wide * wide
        norm_ref[i * chunk : (i + 1) * chunk, :] = total


def load(index, x, width):
    rows, features = x.shape
    part = (rows // PARTS, features // 2)
    return pl.pallas_call(
        functools.partial(load_kernel, width),
        in_specs=[SMEM, ANY],
        out_specs=[VMEM] * (2 + PARTS),
        out_shape=[pltpu.VMEM(x.shape, BF16), pltpu.VMEM((rows, 128), F32)] + [pltpu.VMEM(part, BF16)] * PARTS,
        scratch_shapes=[pltpu.SemaphoreType.DMA((LOADS,))],
        compiler_params=PARAMS,
        cost_estimate=pl.CostEstimate(flops=2 * rows * features, bytes_accessed=4 * rows * features, transcendentals=0),
    )(index, pltpu.with_memory_space_constraint(x, pltpu.HBM))


def tokens(index_ref, group_ref, width, entry, j, x_ref, other_refs):
    owner, start, size, flip = entry
    block = jnp.bitwise_xor(index_ref[0], 2 * owner[j])
    if flip is not None:
        start = start + jnp.bitwise_xor(group_ref[0], flip) * size
    mine = x_ref[:, pl.ds(pl.multiple_of(block * width + start, 128), size)]
    where = pl.ds(pl.multiple_of(block // 2 * width + start, 128), size)
    return jnp.concatenate([mine] + [ref[:, where] for ref in other_refs], axis=0)


def project_kernel(width, entries, has_init, index_ref, group_ref, x_ref, *refs):
    others, refs, out_ref = refs[:PARTS], refs[PARTS:-1], refs[-1]
    total = refs[len(entries)][...] if has_init else None
    for j in range(4):
        left = [tokens(index_ref, group_ref, width, entry, j, x_ref, others) for entry in entries]
        block = [ref[j * entry[2] : (j + 1) * entry[2], :] for ref, entry in zip(refs, entries)]
        term = jnp.dot(
            jnp.concatenate(left, axis=1), jnp.concatenate(block, axis=0), preferred_element_type=F32
        )
        total = term if total is None else total + term
    out_ref[...] = total


def project(place, entries, x, others, arrays, init=None):
    index, group, width = place
    rows, rank = x.shape[0], arrays[0].shape[1]
    depth = sum(array.shape[0] for array in arrays)
    extra = [] if init is None else [init]
    return pl.pallas_call(
        functools.partial(project_kernel, width, entries, init is not None),
        in_specs=[SMEM] * 2 + [VMEM] * (1 + PARTS + len(arrays) + len(extra)),
        out_specs=VMEM,
        out_shape=jax.ShapeDtypeStruct((2 * rows, rank), F32),
        compiler_params=PARAMS,
        cost_estimate=pl.CostEstimate(
            flops=4 * rows * depth * rank, bytes_accessed=4 * rows * depth, transcendentals=0
        ),
    )(index, group, pinned(x), *map(pinned, others), *arrays, *extra)


def spread_kernel(width, entries, coded, index_ref, group_ref, x_ref, *refs):
    others, y_ref, outs = refs[:PARTS], refs[PARTS], refs[PARTS + 1 :]
    turned = y_ref[...].astype(F32).T.astype(BF16)
    for out, entry in zip(outs, entries):
        size = entry[2]
        for j in range(4):
            right = tokens(index_ref, group_ref, width, entry, j, x_ref, others)
            term = jnp.dot(turned, right, preferred_element_type=F32).T
            out[j * size : (j + 1) * size, :] = encode(term) if coded else term


def spread(place, entries, coded, x, others, y):
    index, group, width = place
    rows, rank = x.shape[0], y.shape[1]
    sizes = [entry[2] for entry in entries]
    return pl.pallas_call(
        functools.partial(spread_kernel, width, entries, coded),
        in_specs=[SMEM] * 2 + [VMEM] * (2 + PARTS),
        out_specs=[VMEM] * len(sizes),
        out_shape=[jax.ShapeDtypeStruct((4 * size, rank), BF16 if coded else F32) for size in sizes],
        compiler_params=PARAMS,
        cost_estimate=pl.CostEstimate(
            flops=16 * rows * sum(sizes) * rank, bytes_accessed=16 * rows * sum(sizes), transcendentals=0
        ),
    )(index, group, pinned(x), *map(pinned, others), y)


def factor_kernel(scale, gram_ref, range_ref, out_ref, basis_ref):
    n, b = gram_ref.shape[0], 8
    lane = lax.broadcasted_iota(jnp.int32, (b, n), 1)
    sub = lax.broadcasted_iota(jnp.int32, (b, n), 0)

    def full(value):
        return jnp.broadcast_to(value, (b, n))

    tiles = [gram_ref[b * i : b * i + b, :] for i in range(n // b)]
    for t in range(n // b):
        k = b * t
        group = (lane >= k) & (lane < k + b)
        cols = [full(tiles[t][:, k + c : k + c + 1]) for c in range(b)]
        entry = {(r, c): full(cols[c][r : r + 1, :]) for r in range(b) for c in range(r + 1)}
        rows = [jnp.where(lane == k + r, 1.0, jnp.where(group, 0.0, full(tiles[t][r : r + 1, :]))) for r in range(b)]
        invs, low = [], {}
        for c in range(b):
            invs.append(1.0 / entry[c, c])
            for r in range(c + 1, b):
                low[r, c] = entry[r, c] * invs[c]
            for r in range(c + 1, b):
                for s in range(c + 1, r + 1):
                    entry[r, s] = entry[r, s] - low[r, c] * entry[s, c]
            for r in range(c + 1, b):
                rows[r] = rows[r] - low[r, c] * rows[c]
        solved = [row * inv for row, inv in zip(rows, invs)]
        for c in range(b - 1, 0, -1):
            for r in range(c):
                solved[r] = solved[r] - low[c, r] * solved[c]
        for i in range(t + 1, n // b):
            new = jnp.where(group, 0.0, tiles[i])
            for c in range(b):
                new = new - full(tiles[i][:, k + c : k + c + 1]) * solved[c]
            tiles[i] = new
        done, pivots = rows[0], entry[0, 0]
        for r in range(1, b):
            done = jnp.where(sub == r, rows[r], done)
            pivots = jnp.where(sub == r, entry[r, r], pivots)
        out_ref[k : k + b, :] = jnp.where(lane <= k + sub, done, 0.0) * lax.rsqrt(pivots)
    basis_ref[...] = scale * lax.dot_general(
        range_ref[...], out_ref[...], (((1,), (1,)), ((), ())), precision=HIGH, preferred_element_type=F32
    )


def factored(scale, gram, range_rows):
    return pl.pallas_call(
        functools.partial(factor_kernel, scale),
        in_specs=[VMEM] * 2,
        out_specs=[VMEM] * 2,
        out_shape=[jax.ShapeDtypeStruct(gram.shape, F32), jax.ShapeDtypeStruct(range_rows.shape, F32)],
        compiler_params=PARAMS,
        cost_estimate=pl.CostEstimate(flops=10**7, bytes_accessed=2 * 10**7, transcendentals=0),
    )(gram, range_rows)


def close_kernel(depth, part_ref, theirs_ref, inverse_ref, norm_ref, coords_ref, resid_ref):
    raw = part_ref[: theirs_ref.shape[0], :] + theirs_ref[...]
    coords = lax.dot_general(raw, inverse_ref[...], (((1,), (1,)), ((), ())), precision=HIGH)
    coords_ref[...] = coords
    lost = coords - coords.astype(BF16).astype(F32)
    terms = norm_ref[...] + (lost * lost - coords * coords)
    energy = jnp.sum(terms.T, axis=0, keepdims=True)
    resid_ref[...] = jnp.sqrt(jnp.maximum(energy, 0.0) / depth + 1e-06)


def close(depth, part, theirs, inverse, norm):
    rows, rank = theirs.shape
    return pl.pallas_call(
        functools.partial(close_kernel, depth),
        in_specs=[VMEM] * 4,
        out_specs=[VMEM] * 2,
        out_shape=[jax.ShapeDtypeStruct((rows, rank), F32), jax.ShapeDtypeStruct((1, rows), F32)],
        compiler_params=PARAMS,
        cost_estimate=pl.CostEstimate(flops=2 * rows * rank * rank, bytes_accessed=16 * rows * rank, transcendentals=0),
    )(part, theirs, inverse, norm)


def shards(n, activations, sketch):
    x, rows = activations, activations.shape[0]
    width, rank = sketch.shape[1:]
    depth = n * width
    index, group = (lax.axis_index(axis).astype(jnp.int32).reshape(1) for axis in ("tok", "groups"))
    place = (index, group, width)

    def across(value):
        return lax.ppermute(value, "groups", [(0, 1), (1, 0)])

    with jax.named_scope("gather_sketch"):
        pieces = layout(width, SKETCH_PIECES)
        held = []
        for (start, size, _), (_, _, shared) in zip(pieces, SKETCH_PIECES):
            first = start + (group[0] * size if shared else 0)
            held.append(lax.dynamic_slice(sketch[0], (first, 0), (size, rank)))
        came = [swap(held[p], 2 * order[0], n) for p, (_, order, _) in enumerate(SKETCH_PIECES)]
    with jax.named_scope("split_features"):
        x, norm, *others = load(index, x, width)
        others = lax.optimization_barrier((*others, *came[:TIED]))[:PARTS]
        others = [swap(part, 1, n) for part in others]
    with jax.named_scope("gather_sketch"):
        near, near_rows, far, far_rows = [], [], [], []
        for p, (share, order, shared) in enumerate(SKETCH_PIECES):
            start, size, (near_owners, far_owners) = pieces[p]
            own = 0 if shared else None
            first = jnp.concatenate([held[p], came[p]])
            array = jnp.concatenate([first, swap(first, 2 * order[1], n)])
            last = swap(array, 2 * order[2], n)
            near.append(array)
            near_rows.append((near_owners, start, size, own))
            far.append(last)
            far_rows.append((far_owners, start, size, own))
            if shared:
                far += [across(array), across(last)]
                far_rows += [(near_owners, start, size, 1), (far_owners, start, size, 1)]
    with jax.named_scope("sketched"):
        part = project(place, near_rows, x, others, near)
        early = [i for i in range(len(far)) if i != LAST]
        part = project(place, [far_rows[i] for i in early], x, others, [far[i] for i in early], part)
        part = project(place, far_rows[LAST : LAST + 1], x, others, far[LAST : LAST + 1], part)
        theirs = swap(part, 1, n)
        sketched = (part + jnp.concatenate([theirs[rows:], theirs[:rows]])).astype(BF16)
    with jax.named_scope("range"):
        orders = [order for _, order, _ in RANGE_PIECES]
        every = range(len(orders))
        pieces = layout(width, RANGE_PIECES)
        near_rows = [(near_owners, start, size, None) for start, size, (near_owners, _) in pieces]
        far_rows = [(far_owners, start, size, None) for start, size, (_, far_owners) in pieces]
        sent = spread(place, far_rows, True, x, others, sketched)
        kept = spread(place, near_rows, False, x, others, sketched)
        sums, held = [], []
        for p in every:
            mine, coded = kept[p], sent[p]
            for bit in orders[p][:0:-1]:
                total = mine + decode(swap(coded, 2 * bit, n))
                cut = total.shape[0] // 2
                mine, coded = total[:cut], encode(total[cut:])
            theirs = decode(swap(encode(total), 2 * orders[p][0], n))
            own = total[:cut] + theirs[cut:]
            sums.append(own)
            held.append(jnp.concatenate([own, total[cut:] + theirs[:cut]]).astype(BF16))
        range_rows = jnp.concatenate(sums, axis=0)
    with jax.named_scope("gather_range"):
        came = [swap(held[p], 2 * orders[p][1], n) for p in every]
    with jax.named_scope("gram"):
        gram = jnp.dot(range_rows.T, range_rows, preferred_element_type=F32, precision=HIGH)
        for bit in (1, 2):
            gram = gram + swap(gram, bit, n)
        gram = after(gram, came[0])
        apart = [swap(gram, bit, n) for bit in (4, 8, 12)]
        gram = (gram + apart[0]) + (apart[1] + apart[2])
    with jax.named_scope("gather_range"):
        held = [jnp.concatenate([held[p], came[p]]) for p in every]
        came = [swap(held[p], 2 * orders[p][2], n) for p in every]
    with jax.named_scope("factor"):
        inverse, basis = factored(math.sqrt(depth), gram, range_rows)
    with jax.named_scope("coords"):
        part = project(place, near_rows, x, others, held)
        part = project(place, far_rows, x, others, came, after(part, inverse))
        coords, resid_rms = close(depth, part, swap(part[rows:], 1, n), inverse, norm)
    return basis[None], coords, resid_rms.reshape(rows)


def shards_any(depth, activations, sketch):
    sketch_all = lax.all_gather(sketch, "tok", axis=1, tiled=True)[0]
    sketched = lax.psum(jnp.dot(activations, sketch_all, preferred_element_type=F32), "feat").astype(BF16)
    term = lax.dot_general(activations, sketched, (((0,), (0,)), ((), ())), preferred_element_type=F32)
    range_rows = lax.psum_scatter(term, "tok", scatter_dimension=0, tiled=True)
    gram = jnp.dot(range_rows.T, range_rows, preferred_element_type=F32, precision=HIGH)
    factor = jnp.linalg.cholesky(lax.psum(gram, ("tok", "feat")))
    own_rows = jax.scipy.linalg.solve_triangular(factor, range_rows.T, lower=True).T
    half_basis = lax.all_gather(own_rows.astype(BF16), "tok", axis=0, tiled=True)
    basis = (own_rows * F32(math.sqrt(depth)))[None]
    coords = lax.psum(jnp.dot(activations, half_basis, preferred_element_type=F32), "feat")
    rebuilt = jnp.dot(coords.astype(BF16), half_basis.T, preferred_element_type=F32)
    leftover = activations.astype(F32) - rebuilt
    energy = lax.psum(jnp.sum(leftover * leftover, axis=1), "feat")
    return basis, coords, jnp.sqrt(energy / depth + 1e-06)


def solution(mesh):
    n, feat = mesh.shape["tok"], mesh.shape["feat"]

    def call(activations, sketch):
        depth = activations.shape[1]
        if n == 16 and feat == 1:
            body = functools.partial(shards, n)
        else:
            body = functools.partial(shards_any, depth)
        return jax.shard_map(
            body,
            mesh=mesh,
            in_specs=(P(("groups", "tok"), "feat"), P("feat", "tok", None)),
            out_specs=(
                P(("groups", "feat"), "tok", None),
                P(("groups", "tok"), None),
                P(("groups", "tok")),
            ),
            check_vma=False,
        )(activations, sketch)

    return call
```
